256 devices in a mesh: gz: 32 (over x, z), gy: 8 (over y, core).
Axes of the slice: x: 4, y: 4, z: 8, core: 2. Of those that a mesh axis runs over, the one named last changes fastest.
Arguments:
- spectrum: float32 [3, 2, 4, 1024, 4096], P(None, None, None, 'gy', 'gz'), may hold values from -6 to 6
- cells: int32 [2, 524288], P(None, ('gz', 'gy')), may hold values from 0 to 4095, as said below
- offsets: float32 [3, 524288], P(None, ('gz', 'gy')), may hold values from 0 to 1
- counts: int32 [256], P(('gz', 'gy')), may hold values from 1 to 2048, as said below
Outputs:
- coefficients: float32 [3, 4, 1024, 4096], P(None, None, 'gy', 'gz')
- interpolated: float32 [3, 524288], P(None, ('gz', 'gy'))
The draws below stay inside these ranges and needn't reach their ends.
Inputs may be any that keep to these rules, and one draw needn't show every extreme that they name: The particles of device number b = i * (size of gy) + j, at gz index i and gy index j, occupy slots b * 2048 to b * 2048 + 2047. Their base cells lie from two cells before that device's block to the cell just after its last one: along y from j * 128 - 2 to j * 128 + 128 modulo 1024, along z from i * 128 - 2 to i * 128 + 128 modulo 4096. Empty slots hold such cells too. `counts`: live particles of each device fill its first slots; some device has exactly 2048.
All inputs are finite; a program needn't handle non-finite values.
Results may differ from the reference program's by a relative error of at most 0.000096.
Values sent between devices are 32-bit elements; how exact they have to be, the bound alone decides.
No kernel may reach another device: no remote copies, remote signals or barrier semaphores. Data moves between devices by JAX's collectives and lax.ppermute only.
A program may use at most 64 MiB of HBM per device.

```python
import math
import jax
import jax.numpy as jnp

NZ = 4096
COMPS = 3
NX = 4
CY = 128
PCAP = 2048
NY = 1024
CZ = 128
NDEV = 256
SLOTS = 524288
N_GY = 8


def draw_cells(key, part):
    slot = jnp.arange(SLOTS, dtype=jnp.int32)
    owner = slot // PCAP
    owner_z = owner // N_GY
    owner_y = owner % N_GY
    key_y, key_z = jax.random.split(key)
    shift_y = jax.random.randint(key_y, (SLOTS,), -2, CY + 1, dtype=jnp.int32)
    shift_z = jax.random.randint(key_z, (SLOTS,), -2, CZ + 1, dtype=jnp.int32)
    cell_y = (owner_y * CY + shift_y) % NY
    cell_z = (owner_z * CZ + shift_z) % NZ
    return jnp.stack([cell_y, cell_z]).astype(jnp.int32)


def draw_counts(key, part):
    key_div, key_jit, key_top = jax.random.split(key, 3)
    divisor = jax.random.randint(key_div, (NDEV,), 1, 5, dtype=jnp.int32)
    jitter = jax.random.randint(key_jit, (NDEV,), 0, max(PCAP // 16, 1), dtype=jnp.int32)
    basic = jnp.maximum(PCAP // divisor - jitter, 1)
    fullest = jax.random.randint(key_top, (), 0, NDEV, dtype=jnp.int32)
    return jnp.where(jnp.arange(NDEV, dtype=jnp.int32) == fullest, PCAP, basic).astype(jnp.int32)


def block_levels(stream_key, dims, pieces, low, top_value):
    loudness = 1.0
    for dim, parts in pieces:
        steps = jax.random.uniform(jax.random.fold_in(jax.random.fold_in(stream_key, 6), dim), (parts,), jnp.float32, low / len(pieces), top_value / len(pieces))
        loudness = loudness * jnp.repeat(jnp.exp(steps), dims[dim] // parts).reshape((-1,) + (1,) * (len(dims) - 1 - dim))
    return loudness


def noise(own_key, dims, scale, reach, cuts=(), held_as=jnp.bfloat16):
    factor_of = block_levels(own_key, dims, cuts, -0.22, 0.18) if cuts else 1.0
    drawn = jax.random.normal(own_key, dims, jnp.float32) * scale * factor_of
    return jnp.minimum(jnp.maximum(drawn, -reach), reach).astype(held_as)


def setup_inputs(seed: int = 0) -> dict:
    splits = jax.random.split(jax.random.key(seed), 5)
    return {
        "spectrum": noise(splits[0], (COMPS, 2, NX, NY, NZ), 1.0, 6.0, ((3, 8), (4, 32)), jnp.float32),
        "cells": draw_cells(jax.random.fold_in(splits[4], 71), 0),
        "offsets": jnp.clip(1.0 * jax.random.uniform(splits[2], (3, SLOTS), jnp.float32) ** block_levels(splits[2], (3, SLOTS), ((1, 256),), -0.2, 0.2), 0.0, 1.0),
        "counts": draw_counts(jax.random.fold_in(splits[4], 71), 0),
    }


def spline_weights(frac):
    cube = frac * frac * frac
    square = frac * frac
    first = (1.0 - frac) * (1.0 - frac) * (1.0 - frac) / 6.0
    second = (3.0 * cube - 6.0 * square + 4.0) / 6.0
    third = (-3.0 * cube + 3.0 * square + 3.0 * frac + 1.0) / 6.0
    fourth = cube / 6.0
    return [first, second, third, fourth]

def reference(spectrum, cells, offsets, counts):
    wave = jnp.arange(NZ).astype(spectrum.dtype)
    symbol = (4.0 + 2.0 * jnp.cos(wave * (2.0 * math.pi / NZ))) / 6.0
    factor = 1.0 / (symbol * math.sqrt(NZ))
    real_part = spectrum[:, 0] * factor
    imag_part = spectrum[:, 1] * factor
    complex_hat = real_part + 1j * imag_part
    coefficients = jnp.real(jnp.fft.ifft(complex_hat, axis=-1)) * NZ
    coefficients = coefficients.astype(spectrum.dtype)
    weight_x = spline_weights(offsets[0])
    weight_y = spline_weights(offsets[1])
    weight_z = spline_weights(offsets[2])
    total_sum = jnp.zeros((COMPS, NX, SLOTS), spectrum.dtype)
    for step_y in range(4):
        index_y = ((cells[0] - 1 + step_y) % NY).astype(jnp.int32)
        for step_z in range(4):
            index_z = ((cells[1] - 1 + step_z) % NZ).astype(jnp.int32)
            picked = coefficients[:, :, index_y, index_z]
            total_sum = total_sum + picked * (weight_y[step_y] * weight_z[step_z])[None, None, :]
    values = total_sum[:, 0] * weight_x[0]
    for plane in range(1, 4):
        values = values + total_sum[:, plane] * weight_x[plane]
    slot = jnp.arange(SLOTS, dtype=jnp.int32)
    live_mask = slot % PCAP < counts[slot // PCAP]
    interpolated = jnp.where(live_mask[None, :], values, jnp.zeros_like(values))
    return (coefficients, interpolated)
```

```python
import math

import jax
import jax.numpy as jnp
import numpy as np
from jax import lax
from jax.experimental import pallas as pl
from jax.experimental.pallas import tpu as pltpu
from jax.sharding import PartitionSpec as P

GROUP = 32
CELLS = 128
LINES = 48
SENT = 56
TILE = 256
VMEM = 48 * 1024 * 1024


def split(value):
    high = value.astype(jnp.bfloat16)
    low = (value - high.astype(jnp.float32)).astype(jnp.bfloat16)
    return high, low


def tables():
    length = GROUP * CELLS
    place = np.arange(length, dtype=np.float64).reshape(GROUP, CELLS)
    symbol = (4.0 + 2.0 * np.cos(2.0 * np.pi * place / length)) / 6.0
    scale = 1.0 / (symbol * math.sqrt(length))
    twist = 2.0 * np.pi * np.outer(np.arange(GROUP), np.arange(CELLS)) / length
    columns = np.arange(CELLS)
    outer = 4 * (columns % GROUP) + columns // GROUP
    last = 2.0 * np.pi * (np.outer(np.arange(CELLS), outer) % CELLS) / CELLS
    matrix = np.concatenate([np.cos(last), -np.sin(last)], axis=0).astype(np.float32)
    high = matrix.astype(jnp.bfloat16)
    low = (matrix - high.astype(np.float32)).astype(jnp.bfloat16)
    return (
        np.stack([scale, np.cos(twist), np.sin(twist)]).astype(np.float32),
        np.concatenate([high, low, high], axis=0),
    )


def add(one, two):
    return one[0] + two[0], one[1] + two[1]


def sub(one, two):
    return one[0] - two[0], one[1] - two[1]


def by_i(one):
    return -one[1], one[0]


def turn(one, part, whole):
    part = part % whole
    if part == 0:
        return one
    if 4 * part == whole:
        return by_i(one)
    if 2 * part == whole:
        return -one[0], -one[1]
    if 4 * part == 3 * whole:
        return one[1], -one[0]
    cos = math.cos(2.0 * math.pi * part / whole)
    sin = math.sin(2.0 * math.pi * part / whole)
    if 8 * part == whole:
        return (one[0] - one[1]) * cos, (one[0] + one[1]) * cos
    if 8 * part == 3 * whole:
        return (one[0] + one[1]) * cos, (one[1] - one[0]) * cos
    return one[0] * cos - one[1] * sin, one[0] * sin + one[1] * cos


def dft4(a, b, c, d):
    even, odd = add(a, c), sub(a, c)
    both, diff = add(b, d), by_i(sub(b, d))
    return [add(even, both), add(odd, diff), sub(even, both), sub(odd, diff)]


def dft8(items):
    even = dft4(*items[0::2])
    odd = dft4(*items[1::2])
    odd = [turn(item, place, 8) for place, item in enumerate(odd)]
    return [add(e, o) for e, o in zip(even, odd)] + [sub(e, o) for e, o in zip(even, odd)]


def dft32(items):
    firsts = []
    for j in range(8):
        four = dft4(items[j], items[j + 8], items[j + 16], items[j + 24])
        firsts.append([turn(item, j * r, 32) for r, item in enumerate(four)])
    out = [None] * 32
    for r in range(4):
        for q, item in enumerate(dft8([firsts[j][r] for j in range(8)])):
            out[r + 4 * q] = item
    return out


def lines_kernel(data, table, matrix, out, wide, flat):
    def columns(index, carry):
        base = pl.multiple_of(index // 2 * 32 + index % 2 * 8, 8)
        base_imag = pl.multiple_of(base + 16, 8)
        items = []
        for k1 in range(GROUP):
            scale = table[0, k1 : k1 + 1, :]
            items.append(
                (data[k1, pl.ds(base, 8), :] * scale, data[k1, pl.ds(base_imag, 8), :] * scale)
            )
        pair = []
        for m, item in enumerate(dft32(items)):
            cos, sin = table[1, m : m + 1, :], table[2, m : m + 1, :]
            pair.append((item[0] * cos - item[1] * sin, item[0] * sin + item[1] * cos))
            if m % 2 == 1:
                row = pl.multiple_of(index * 256 + m * 8 - 8, 16)
                real, imag = [jnp.concatenate(parts, axis=0) for parts in zip(*pair)]
                fill(wide, row, 16, real, imag)
                pair = []
        return carry

    lax.fori_loop(0, 6, columns, 0)
    flat[...] = jnp.dot(wide[...], matrix[...], preferred_element_type=jnp.float32)
    lane = lax.broadcasted_iota(jnp.int32, (GROUP, CELLS), 1)
    odd = lane // 32 % 2 == 1
    upper = lane // 64 == 1
    for index in range(6):
        for half in range(2):
            rows = [
                flat[pl.ds(index * 256 + half * 4 + line, GROUP, stride=8), :]
                for line in range(4)
            ]
            turned = jnp.concatenate(rows, axis=0).T
            v = [turned[s * 32 : s * 32 + 32] for s in range(4)]
            w = [
                jnp.where(odd, pltpu.roll(v[1], 32, 1), v[0]),
                jnp.where(odd, v[1], pltpu.roll(v[0], 96, 1)),
                jnp.where(odd, pltpu.roll(v[3], 32, 1), v[2]),
                jnp.where(odd, v[3], pltpu.roll(v[2], 96, 1)),
            ]
            o = [
                jnp.where(upper, pltpu.roll(w[2], 64, 1), w[0]),
                jnp.where(upper, pltpu.roll(w[3], 64, 1), w[1]),
                jnp.where(upper, w[2], pltpu.roll(w[0], 64, 1)),
                jnp.where(upper, w[3], pltpu.roll(w[1], 64, 1)),
            ]
            for line in range(4):
                row = index * 8 + half * 4 + line
                out[pl.ds(row, GROUP, stride=SENT), :] = o[line]
    empty = jnp.zeros((CELLS - LINES, CELLS), jnp.float32)
    for edge in range(6):
        m = 29 + edge if edge < 3 else edge - 3
        rows = [flat[index * 256 + m * 8 : index * 256 + m * 8 + 8, :] for index in range(6)]
        turned = jnp.concatenate(rows + [empty], axis=0).T
        if edge < 3:
            moved = pltpu.roll(turned[96:128], 1, 0)
        else:
            moved = pltpu.roll(turned[0:32], 31, 0)
        out[pl.ds(LINES + edge, GROUP, stride=SENT), :] = moved
    blank = jnp.zeros((GROUP, CELLS), jnp.float32)
    for edge in range(6, 8):
        out[pl.ds(LINES + edge, GROUP, stride=SENT), :] = blank


def transform(received):
    numbers, matrix = tables()
    return pl.pallas_call(
        lines_kernel,
        out_shape=jax.ShapeDtypeStruct((GROUP * SENT, CELLS), jnp.float32),
        scratch_shapes=[
            pltpu.VMEM((GROUP * LINES, 768), jnp.bfloat16),
            pltpu.VMEM((GROUP * LINES, CELLS), jnp.float32),
        ],
        compiler_params=pltpu.CompilerParams(vmem_limit_bytes=VMEM),
        name="lines",
    )(received, jnp.asarray(numbers), jnp.asarray(matrix))


def spline_weights(frac):
    cube = frac * frac * frac
    square = frac * frac
    rest = 1.0 - frac
    return [
        rest * rest * rest / 6.0,
        (3.0 * cube - 6.0 * square + 4.0) / 6.0,
        (-3.0 * cube + 3.0 * square + 3.0 * frac + 1.0) / 6.0,
        cube / 6.0,
    ]


def spread(weights, step):
    out = jnp.where(step == 0, weights[0], 0.0)
    for place in range(1, 4):
        out = jnp.where(step == place, weights[place], out)
    return out


def particle_tile(start, cells, offsets, at, length_y, length_z):
    spot = pl.ds(at, TILE)
    first_y = ((cells[0:1, spot] - start[0] + 2) & (length_y - 1)) - 3
    first_z = ((cells[1:2, spot] - start[1] + 2) & (length_z - 1)) - 3
    weights = [spline_weights(offsets[d : d + 1, spot]) for d in range(3)]
    row = lax.broadcasted_iota(jnp.int32, (CELLS, TILE), 0)
    inner = spread(weights[2], row - first_z)
    edge = lax.broadcasted_iota(jnp.int32, (8, TILE), 0)
    edge = jnp.where(edge < 3, edge - 3, jnp.where(edge < 6, edge + 125, -9999))
    outer = spread(weights[2], edge - first_z)
    full = jnp.concatenate([inner] + [outer] * 16, axis=0)
    return first_y, weights, full


def fill(wide, row, count, inner, outer):
    for at, part in ((0, inner), (CELLS, outer)):
        high, low = split(part)
        wide[pl.ds(row, count), at : at + CELLS] = high
        wide[pl.ds(row, count), at + 256 : at + 256 + CELLS] = high
        wide[pl.ds(row, count), at + 512 : at + 512 + CELLS] = low


def fill_weights(near, full):
    high, low = split(full)
    near[0:256, :] = high
    near[256:512, :] = low
    near[512:768, :] = high


def block_kernel(lengths, start, data, cells, offsets, coefficients, sums, wide, near, held):
    lane = lax.broadcasted_iota(jnp.int32, (LINES, CELLS), 1)
    for group in range(2):
        tails = [data[group * 16 + t, LINES:SENT, :] for t in range(16)]
        turned = jnp.concatenate(tails, axis=0).T[:LINES]
        for t in range(16):
            whole = group * 16 + t
            inner = data[whole, :LINES, :]
            fill(wide, whole * LINES, LINES, inner, jnp.where(lane // 8 == t, turned, 0.0))
            for c in range(3):
                coefficients[c, whole // 8, whole % 8 * 16 : whole % 8 * 16 + 16, :] = inner[
                    c * 16 : c * 16 + 16
                ]

    def tile(index, carry):
        at = pl.multiple_of(index * TILE, TILE)
        first_y, weights, full = particle_tile(start, cells, offsets, at, *lengths)
        fill_weights(near, full)
        held[...] = jnp.dot(wide[...], near[...], preferred_element_type=jnp.float32)
        row = lax.broadcasted_iota(jnp.int32, (8, TILE), 0)
        totals = [[None] * 3 for _ in range(4)]
        for part in range(16):
            side = spread(weights[1], row + (part * 8) - first_y)
            for a in range(4):
                for c in range(3):
                    place = (a * 8 + part // 2) * LINES + c * 16 + part % 2 * 8
                    term = held[place : place + 8, :] * side
                    total = totals[a][c]
                    totals[a][c] = term if total is None else total + term
        for c in range(3):
            total = totals[0][c] * weights[0][0]
            for a in range(1, 4):
                total = total + totals[a][c] * weights[0][a]
            sums[c : c + 1, pl.ds(at, TILE)] = jnp.sum(total, axis=0, keepdims=True)
        return carry

    lax.fori_loop(0, cells.shape[1] // TILE, tile, 0)


def edge_kernel(lengths, start, below, above, cells, offsets, sums, out, wide, near, held):
    lane = lax.broadcasted_iota(jnp.int32, (8, CELLS), 1)
    sides = (below, above)
    tails = [sides[place // 4][place % 4, 24:32, :] for place in range(8)]
    blank = jnp.zeros((64, CELLS), jnp.float32)
    turned = jnp.concatenate(tails + [blank], axis=0).T
    for place in range(8):
        for c in range(3):
            inner = sides[place // 4][place % 4, c * 8 : c * 8 + 8, :]
            first = c * 16 + (8 if place < 4 else 0)
            outer = jnp.where(lane // 8 == place, turned[first : first + 8], 0.0)
            held[(place * 3 + c) * 8 : (place * 3 + c) * 8 + 8, :CELLS] = inner
            held[(place * 3 + c) * 8 : (place * 3 + c) * 8 + 8, CELLS:] = outer
    fill(wide, 0, 192, held[:, :CELLS], held[:, CELLS:])

    def tile(index, carry):
        at = pl.multiple_of(index * TILE, TILE)
        first_y, weights, full = particle_tile(start, cells, offsets, at, *lengths)
        fill_weights(near, full)
        held[...] = jnp.dot(wide[...], near[...], preferred_element_type=jnp.float32)
        row = lax.broadcasted_iota(jnp.int32, (8, TILE), 0)
        low = spread(weights[1], row - 8 - first_y)
        high = spread(weights[1], row + CELLS - first_y)
        slot = at + lax.broadcasted_iota(jnp.int32, (1, TILE), 1)
        for c in range(3):
            total = None
            for a in range(4):
                term = (
                    held[(a * 3 + c) * 8 : (a * 3 + c) * 8 + 8, :] * low
                    + held[((a + 4) * 3 + c) * 8 : ((a + 4) * 3 + c) * 8 + 8, :] * high
                ) * weights[0][a]
                total = term if total is None else total + term
            value = sums[c : c + 1, pl.ds(at, TILE)] + jnp.sum(total, axis=0, keepdims=True)
            out[c : c + 1, pl.ds(at, TILE)] = jnp.where(slot < start[2], value, 0.0)
        return carry

    lax.fori_loop(0, cells.shape[1] // TILE, tile, 0)


def vmem():
    return pl.BlockSpec(memory_space=pltpu.VMEM)


def interpolate_block(lengths, start, data, cells, offsets):
    def body(*refs):
        block_kernel(lengths, *refs)

    slots = cells.shape[1]
    return pl.pallas_call(
        body,
        in_specs=[pl.BlockSpec(memory_space=pltpu.SMEM)] + [vmem()] * 3,
        out_specs=[vmem()] * 2,
        out_shape=[
            jax.ShapeDtypeStruct((3, 4, CELLS, CELLS), jnp.float32),
            jax.ShapeDtypeStruct((3, slots), jnp.float32),
        ],
        scratch_shapes=[
            pltpu.VMEM((GROUP * LINES, 768), jnp.bfloat16),
            pltpu.VMEM((768, TILE), jnp.bfloat16),
            pltpu.VMEM((GROUP * LINES, TILE), jnp.float32),
        ],
        compiler_params=pltpu.CompilerParams(vmem_limit_bytes=VMEM),
        cost_estimate=pl.CostEstimate(
            flops=2 * 1536 * 768 * 2048, bytes_accessed=2_000_000, transcendentals=0
        ),
        name="block",
    )(start, data, cells, offsets)


def interpolate_edges(lengths, start, below, above, cells, offsets, sums):
    def body(*refs):
        edge_kernel(lengths, *refs)

    return pl.pallas_call(
        body,
        in_specs=[pl.BlockSpec(memory_space=pltpu.SMEM)] + [vmem()] * 5,
        out_specs=vmem(),
        out_shape=jax.ShapeDtypeStruct(sums.shape, jnp.float32),
        scratch_shapes=[
            pltpu.VMEM((192, 768), jnp.bfloat16),
            pltpu.VMEM((768, TILE), jnp.bfloat16),
            pltpu.VMEM((192, TILE), jnp.float32),
        ],
        compiler_params=pltpu.CompilerParams(vmem_limit_bytes=VMEM),
        name="edges",
    )(start, below, above, cells, offsets, sums)


def per_device(spectrum, cells, offsets, counts):
    rows_y, rows_z = spectrum.shape[3], spectrum.shape[4]
    count_y, count_z = lax.axis_size("gy"), lax.axis_size("gz")
    lengths = (rows_y * count_y, rows_z * count_z)
    start = jnp.stack(
        [lax.axis_index("gy") * rows_y, lax.axis_index("gz") * rows_z, counts[0]]
    ).astype(jnp.int32)
    by_target = spectrum.reshape(6, GROUP, 16, CELLS).transpose(1, 0, 2, 3)
    received = lax.all_to_all(
        by_target.reshape(GROUP, 96, CELLS), "gz", split_axis=0, concat_axis=0, tiled=True
    )
    lines = transform(received).reshape(GROUP, SENT, CELLS)
    owned = lax.all_to_all(lines, "gz", split_axis=0, concat_axis=0, tiled=True)
    tiles = owned.reshape(4, 8, 7, 8, CELLS)
    top = jnp.stack([tiles[:, 7, i] for i in (1, 3, 5, 6)], axis=1).reshape(4, 32, CELLS)
    bottom = jnp.stack([tiles[:, 0, i] for i in (0, 2, 4, 6)], axis=1).reshape(4, 32, CELLS)
    forward = [(i, (i + 1) % count_y) for i in range(count_y)]
    backward = [(target, source) for source, target in forward]
    below = lax.ppermute(top, "gy", forward)
    above = lax.ppermute(bottom, "gy", backward)
    coefficients, sums = interpolate_block(lengths, start, owned, cells, offsets)
    interpolated = interpolate_edges(lengths, start, below, above, cells, offsets, sums)
    return coefficients, interpolated


def solution(mesh):
    placed = (
        P(None, None, None, "gy", "gz"),
        P(None, ("gz", "gy")),
        P(None, ("gz", "gy")),
        P(("gz", "gy")),
    )
    return jax.shard_map(
        per_device,
        mesh=mesh,
        in_specs=placed,
        out_specs=(P(None, None, "gy", "gz"), P(None, ("gz", "gy"))),
        check_vma=False,
    )
```

```python
import math

import jax
import jax.numpy as jnp
import numpy as np
from jax import lax
from jax.experimental import pallas as pl
from jax.experimental.pallas import tpu as pltpu
from jax.sharding import PartitionSpec as P

GROUP = 32
CELLS = 128
LINES = 48
SENT = 56
TILE = 256
MIB = 1024 * 1024


def split(value):
    high = value.astype(jnp.bfloat16)
    low = (value - high.astype(jnp.float32)).astype(jnp.bfloat16)
    return high, low


def tables():
    length = GROUP * CELLS
    place = np.arange(length, dtype=np.float64).reshape(GROUP, CELLS)
    symbol = (4.0 + 2.0 * np.cos(2.0 * np.pi * place / length)) / 6.0
    scale = 1.0 / (symbol * math.sqrt(length))
    twist = 2.0 * np.pi * np.outer(np.arange(GROUP), np.arange(CELLS)) / length
    columns = np.arange(CELLS)
    outer = 4 * (columns % GROUP) + columns // GROUP
    last = 2.0 * np.pi * (np.outer(np.arange(CELLS), outer) % CELLS) / CELLS
    matrix = np.concatenate([np.cos(last), -np.sin(last)], axis=0).astype(np.float32)
    high = matrix.astype(jnp.bfloat16)
    low = (matrix - high.astype(np.float32)).astype(jnp.bfloat16)
    return (
        np.stack([scale, np.cos(twist), np.sin(twist)]).astype(np.float32),
        np.concatenate([high, low, high], axis=0),
    )


def add(one, two):
    return one[0] + two[0], one[1] + two[1]


def sub(one, two):
    return one[0] - two[0], one[1] - two[1]


def by_i(one):
    return -one[1], one[0]


def turn(one, part, whole):
    part = part % whole
    if part == 0:
        return one
    if 4 * part == whole:
        return by_i(one)
    if 2 * part == whole:
        return -one[0], -one[1]
    if 4 * part == 3 * whole:
        return one[1], -one[0]
    cos = math.cos(2.0 * math.pi * part / whole)
    sin = math.sin(2.0 * math.pi * part / whole)
    if 8 * part == whole:
        return (one[0] - one[1]) * cos, (one[0] + one[1]) * cos
    if 8 * part == 3 * whole:
        return (one[0] + one[1]) * cos, (one[1] - one[0]) * cos
    return one[0] * cos - one[1] * sin, one[0] * sin + one[1] * cos


def dft4(a, b, c, d):
    even, odd = add(a, c), sub(a, c)
    both, diff = add(b, d), by_i(sub(b, d))
    return [add(even, both), add(odd, diff), sub(even, both), sub(odd, diff)]


def dft8(items):
    even = dft4(*items[0::2])
    odd = dft4(*items[1::2])
    odd = [turn(item, place, 8) for place, item in enumerate(odd)]
    return [add(e, o) for e, o in zip(even, odd)] + [sub(e, o) for e, o in zip(even, odd)]


def dft32(items):
    firsts = []
    for j in range(8):
        four = dft4(items[j], items[j + 8], items[j + 16], items[j + 24])
        firsts.append([turn(item, j * r, 32) for r, item in enumerate(four)])
    out = [None] * 32
    for r in range(4):
        for q, item in enumerate(dft8([firsts[j][r] for j in range(8)])):
            out[r + 4 * q] = item
    return out


def lines_kernel(data, table, matrix, out, wide, flat):
    def columns(index, carry):
        base = pl.multiple_of(index // 2 * 32 + index % 2 * 8, 8)
        base_imag = pl.multiple_of(base + 16, 8)
        items = []
        for k1 in range(GROUP):
            scale = table[0, k1 : k1 + 1, :]
            items.append(
                (data[k1, pl.ds(base, 8), :] * scale, data[k1, pl.ds(base_imag, 8), :] * scale)
            )
        pair = []
        for m, item in enumerate(dft32(items)):
            cos, sin = table[1, m : m + 1, :], table[2, m : m + 1, :]
            pair.append((item[0] * cos - item[1] * sin, item[0] * sin + item[1] * cos))
            if m % 2 == 1:
                row = pl.multiple_of(index * 256 + m * 8 - 8, 16)
                real, imag = [jnp.concatenate(parts, axis=0) for parts in zip(*pair)]
                for at, part in ((0, real), (CELLS, imag)):
                    high, low = split(part)
                    wide[pl.ds(row, 16), at : at + CELLS] = high
                    wide[pl.ds(row, 16), at + 256 : at + 256 + CELLS] = high
                    wide[pl.ds(row, 16), at + 512 : at + 512 + CELLS] = low
                pair = []
        return carry

    lax.fori_loop(0, 6, columns, 0)
    flat[...] = jnp.dot(wide[...], matrix[...], preferred_element_type=jnp.float32)
    lane = lax.broadcasted_iota(jnp.int32, (GROUP, CELLS), 1)
    odd = lane // 32 % 2 == 1
    upper = lane // 64 == 1
    for index in range(6):
        for half in range(2):
            rows = [
                flat[pl.ds(index * 256 + half * 4 + line, GROUP, stride=8), :]
                for line in range(4)
            ]
            turned = jnp.concatenate(rows, axis=0).T
            v = [turned[s * 32 : s * 32 + 32] for s in range(4)]
            w = [
                jnp.where(odd, pltpu.roll(v[1], 32, 1), v[0]),
                jnp.where(odd, v[1], pltpu.roll(v[0], 96, 1)),
                jnp.where(odd, pltpu.roll(v[3], 32, 1), v[2]),
                jnp.where(odd, v[3], pltpu.roll(v[2], 96, 1)),
            ]
            o = [
                jnp.where(upper, pltpu.roll(w[2], 64, 1), w[0]),
                jnp.where(upper, pltpu.roll(w[3], 64, 1), w[1]),
                jnp.where(upper, w[2], pltpu.roll(w[0], 64, 1)),
                jnp.where(upper, w[3], pltpu.roll(w[1], 64, 1)),
            ]
            for line in range(4):
                row = index * 8 + half * 4 + line
                out[pl.ds(row, GROUP, stride=SENT), :] = o[line]
    empty = jnp.zeros((CELLS - LINES, CELLS), jnp.float32)
    for edge in range(6):
        m = 29 + edge if edge < 3 else edge - 3
        rows = [flat[index * 256 + m * 8 : index * 256 + m * 8 + 8, :] for index in range(6)]
        turned = jnp.concatenate(rows + [empty], axis=0).T
        if edge < 3:
            moved = pltpu.roll(turned[96:128], 1, 0)
        else:
            moved = pltpu.roll(turned[0:32], 31, 0)
        out[pl.ds(LINES + edge, GROUP, stride=SENT), :] = moved
    blank = jnp.zeros((GROUP, CELLS), jnp.float32)
    for edge in range(6, 8):
        out[pl.ds(LINES + edge, GROUP, stride=SENT), :] = blank


def transform(received):
    numbers, matrix = tables()
    return pl.pallas_call(
        lines_kernel,
        out_shape=jax.ShapeDtypeStruct((GROUP * SENT, CELLS), jnp.float32),
        scratch_shapes=[
            pltpu.VMEM((GROUP * LINES, 768), jnp.bfloat16),
            pltpu.VMEM((GROUP * LINES, CELLS), jnp.float32),
        ],
        compiler_params=pltpu.CompilerParams(vmem_limit_bytes=16 * MIB),
        name="lines",
    )(received, jnp.asarray(numbers), jnp.asarray(matrix))


def spline_weights(frac):
    cube = frac * frac * frac
    square = frac * frac
    rest = 1.0 - frac
    return [
        rest * rest * rest / 6.0,
        (3.0 * cube - 6.0 * square + 4.0) / 6.0,
        (-3.0 * cube + 3.0 * square + 3.0 * frac + 1.0) / 6.0,
        cube / 6.0,
    ]


def spread(weights, step):
    out = jnp.where(step == 0, weights[0], 0.0)
    for place in range(1, 4):
        out = jnp.where(step == place, weights[place], out)
    return out


def weights_kernel(lengths, cells, offsets, near, side):
    start_y = lax.axis_index("gy") * CELLS
    start_z = lax.axis_index("gz") * CELLS
    row = lax.broadcasted_iota(jnp.int32, (CELLS, TILE), 0)
    row_y = lax.broadcasted_iota(jnp.int32, (CELLS + 16, TILE), 0) - 8
    edge = lax.broadcasted_iota(jnp.int32, (8, TILE), 0)
    edge = jnp.where(edge < 3, edge - 3, jnp.where(edge < 6, edge + 125, -9999))
    blank = jnp.zeros((8, TILE), jnp.float32)

    def tile(index, carry):
        spot = pl.ds(pl.multiple_of(index * TILE, TILE), TILE)
        first_y = ((cells[0:1, spot] - start_y + 2) & (lengths[0] - 1)) - 3
        first_z = ((cells[1:2, spot] - start_z + 2) & (lengths[1] - 1)) - 3
        weights = [spline_weights(offsets[d : d + 1, spot]) for d in range(3)]
        high, low = split(spread(weights[2], row - first_z))
        near[index, 0:128, :] = high
        near[index, 128:256, :] = high
        near[index, 256:384, :] = low
        outer = spread(weights[2], edge - first_z)
        coarse = outer.astype(jnp.bfloat16).astype(jnp.float32)
        block = jnp.concatenate([coarse, outer - coarse, coarse, blank], axis=0)
        for part in range(4):
            near[index, 384 + part * 32 : 416 + part * 32, :] = block.astype(jnp.bfloat16)
        side[index, 0:144, :] = spread(weights[1], row_y - first_y)
        side[index, 144:152, :] = jnp.concatenate(weights[0] + weights[0], axis=0)
        return carry

    lax.fori_loop(0, cells.shape[1] // TILE, tile, 0)


def fill(wide, row, count, inner, outer):
    high, low = split(inner)
    wide[row : row + count, 0:128] = high
    wide[row : row + count, 128:256] = low
    wide[row : row + count, 256:384] = high
    wide[row : row + count, 384:512] = outer.astype(jnp.bfloat16)


def turn_tails(tails):
    rows = []
    for tail in tails:
        coarse = tail.astype(jnp.bfloat16).astype(jnp.float32)
        rows += [coarse, coarse, tail - coarse, jnp.zeros_like(tail)]
    return jnp.concatenate(rows, axis=0).T


def block_kernel(data, near, side, coefficients, sums, wide, held):
    lane = lax.broadcasted_iota(jnp.int32, (LINES, CELLS), 1)
    for group in range(8):
        turned = turn_tails([data[group * 4 + t, LINES:SENT, :] for t in range(4)])[:LINES]
        for t in range(4):
            whole = group * 4 + t
            inner = data[whole, :LINES, :]
            fill(wide, whole * LINES, LINES, inner, jnp.where(lane // 32 == t, turned, 0.0))
            for c in range(3):
                coefficients[c, whole // 8, whole % 8 * 16 : whole % 8 * 16 + 16, :] = inner[
                    c * 16 : c * 16 + 16
                ]

    def tile(index, slot):
        held[slot] = jnp.dot(wide[...], near[index], preferred_element_type=jnp.float32)
        totals = [[None] * 3 for _ in range(4)]
        for part in range(16):
            weight = side[index, 8 + part * 8 : 16 + part * 8, :]
            for a in range(4):
                for c in range(3):
                    place = (a * 8 + part // 2) * LINES + c * 16 + part % 2 * 8
                    term = held[slot, place : place + 8, :] * weight
                    total = totals[a][c]
                    totals[a][c] = term if total is None else total + term
        for c in range(3):
            total = totals[0][c] * side[index, 144:145, :]
            for a in range(1, 4):
                total = total + totals[a][c] * side[index, 144 + a : 145 + a, :]
            at = index * TILE
            sums[c : c + 1, at : at + TILE] = jnp.sum(total, axis=0, keepdims=True)

    for index in range(near.shape[0]):
        tile(index, index % 2)


def edge_kernel(counts, below, above, near, side, sums, out, wide, held):
    lane = lax.broadcasted_iota(jnp.int32, (16, CELLS), 1)
    sides = (below, above)
    parts = []
    for group in range(2):
        turned = turn_tails([sides[group][a, 24:32, :] for a in range(4)])
        for a in range(4):
            for c in range(3):
                first = c * 16 + (8 if group == 0 else 0)
                outer = jnp.where(lane[:8] // 32 == a, turned[first : first + 8], 0.0)
                parts.append((sides[group][a, c * 8 : c * 8 + 8, :], outer))
    for place in range(0, 24, 2):
        inner, outer = [jnp.concatenate(pair, axis=0) for pair in zip(*parts[place : place + 2])]
        fill(wide, place * 8, 16, inner, outer)
    for index in range(near.shape[0]):
        at = index * TILE
        held[index] = jnp.dot(wide[...], near[index], preferred_element_type=jnp.float32)
        low = side[index, 0:8, :]
        high = side[index, 136:144, :]
        slot = at + lax.broadcasted_iota(jnp.int32, (1, TILE), 1)
        for c in range(3):
            total = None
            for a in range(4):
                term = (
                    held[index, (a * 3 + c) * 8 : (a * 3 + c) * 8 + 8, :] * low
                    + held[index, ((a + 4) * 3 + c) * 8 : ((a + 4) * 3 + c) * 8 + 8, :] * high
                ) * side[index, 144 + a : 145 + a, :]
                total = term if total is None else total + term
            value = sums[c : c + 1, at : at + TILE] + jnp.sum(total, axis=0, keepdims=True)
            out[c : c + 1, at : at + TILE] = jnp.where(slot < counts[0:1, 0:1], value, 0.0)


def vmem():
    return pl.BlockSpec(memory_space=pltpu.VMEM)


def particle_weights(lengths, cells, offsets):
    def body(*refs):
        weights_kernel(lengths, *refs)

    count = cells.shape[1] // TILE
    return pl.pallas_call(
        body,
        in_specs=[vmem()] * 2,
        out_specs=[vmem()] * 2,
        out_shape=[
            jax.ShapeDtypeStruct((count, 512, TILE), jnp.bfloat16),
            jax.ShapeDtypeStruct((count, CELLS + 24, TILE), jnp.float32),
        ],
        compiler_params=pltpu.CompilerParams(vmem_limit_bytes=10 * MIB),
        cost_estimate=pl.CostEstimate(
            flops=10_000_000, bytes_accessed=4_000_000, transcendentals=0
        ),
        name="weights",
    )(cells, offsets)


def interpolate_block(data, near, side):
    count = near.shape[0]
    return pl.pallas_call(
        block_kernel,
        in_specs=[vmem()] * 3,
        out_specs=[vmem()] * 2,
        out_shape=[
            jax.ShapeDtypeStruct((3, 4, CELLS, CELLS), jnp.float32),
            jax.ShapeDtypeStruct((3, count * TILE), jnp.float32),
        ],
        scratch_shapes=[
            pltpu.VMEM((GROUP * LINES, 512), jnp.bfloat16),
            pltpu.VMEM((2, GROUP * LINES, TILE), jnp.float32),
        ],
        compiler_params=pltpu.CompilerParams(vmem_limit_bytes=16 * MIB),
        name="block",
    )(data, near, side)


def interpolate_edges(counts, below, above, near, side, sums):
    return pl.pallas_call(
        edge_kernel,
        in_specs=[vmem()] * 6,
        out_specs=vmem(),
        out_shape=jax.ShapeDtypeStruct(sums.shape, jnp.float32),
        scratch_shapes=[
            pltpu.VMEM((192, 512), jnp.bfloat16),
            pltpu.VMEM((near.shape[0], 192, TILE), jnp.float32),
        ],
        compiler_params=pltpu.CompilerParams(vmem_limit_bytes=10 * MIB),
        name="edges",
    )(counts, below, above, near, side, sums)


def per_device(spectrum, cells, offsets, counts):
    rows_y, rows_z = spectrum.shape[3], spectrum.shape[4]
    count_y, count_z = lax.axis_size("gy"), lax.axis_size("gz")
    lengths = (rows_y * count_y, rows_z * count_z)
    by_target = spectrum.reshape(6, GROUP, 16, CELLS).transpose(1, 0, 2, 3)
    received = lax.all_to_all(
        by_target.reshape(GROUP, 96, CELLS), "gz", split_axis=0, concat_axis=0, tiled=True
    )
    lines = transform(received).reshape(GROUP, SENT, CELLS)
    owned = lax.all_to_all(lines, "gz", split_axis=0, concat_axis=0, tiled=True)
    tiles = owned.reshape(4, 8, 7, 8, CELLS)
    top = jnp.stack([tiles[:, 7, i] for i in (1, 3, 5, 6)], axis=1).reshape(4, 32, CELLS)
    bottom = jnp.stack([tiles[:, 0, i] for i in (0, 2, 4, 6)], axis=1).reshape(4, 32, CELLS)
    forward = [(i, (i + 1) % count_y) for i in range(count_y)]
    backward = [(target, source) for source, target in forward]
    above = lax.ppermute(bottom, "gy", backward)
    below = lax.ppermute(top, "gy", forward)
    near, side = particle_weights(lengths, cells, offsets)
    coefficients, sums = interpolate_block(owned, near, side)
    interpolated = interpolate_edges(counts.reshape(1, 1), below, above, near, side, sums)
    return coefficients, interpolated


def solution(mesh):
    placed = (
        P(None, None, None, "gy", "gz"),
        P(None, ("gz", "gy")),
        P(None, ("gz", "gy")),
        P(("gz", "gy")),
    )
    return jax.shard_map(
        per_device,
        mesh=mesh,
        in_specs=placed,
        out_specs=(P(None, None, "gy", "gz"), P(None, ("gz", "gy"))),
        check_vma=False,
    )
```

```python
import math

import jax
import jax.numpy as jnp
import numpy as np
from jax import lax
from jax.experimental import pallas as pl
from jax.experimental.pallas import tpu as pltpu
from jax.sharding import PartitionSpec as P

GROUP = 32
CELLS = 128
LINES = 48
SENT = 51
TILE = 256
MIB = 1024 * 1024


def split(value):
    high = value.astype(jnp.bfloat16)
    low = (value - high.astype(jnp.float32)).astype(jnp.bfloat16)
    return high, low


def tables():
    length = GROUP * CELLS
    place = np.arange(length, dtype=np.float64).reshape(GROUP, CELLS)
    symbol = (4.0 + 2.0 * np.cos(2.0 * np.pi * place / length)) / 6.0
    scale = 1.0 / (symbol * math.sqrt(length))
    twist = 2.0 * np.pi * np.outer(np.arange(GROUP), np.arange(CELLS)) / length
    columns = np.arange(CELLS)
    outer = 4 * (columns % GROUP) + columns // GROUP
    last = 2.0 * np.pi * (np.outer(np.arange(CELLS), outer) % CELLS) / CELLS
    matrix = np.concatenate([np.cos(last), -np.sin(last)], axis=0).astype(np.float32)
    high = matrix.astype(jnp.bfloat16)
    low = (matrix - high.astype(np.float32)).astype(jnp.bfloat16)
    return (
        np.stack([scale, np.cos(twist), np.sin(twist)]).astype(np.float32),
        np.concatenate([high, low, high], axis=0),
    )


def add(one, two):
    return one[0] + two[0], one[1] + two[1]


def sub(one, two):
    return one[0] - two[0], one[1] - two[1]


def by_i(one):
    return -one[1], one[0]


def turn(one, part, whole):
    part = part % whole
    if part == 0:
        return one
    if 4 * part == whole:
        return by_i(one)
    if 2 * part == whole:
        return -one[0], -one[1]
    if 4 * part == 3 * whole:
        return one[1], -one[0]
    cos = math.cos(2.0 * math.pi * part / whole)
    sin = math.sin(2.0 * math.pi * part / whole)
    if 8 * part == whole:
        return (one[0] - one[1]) * cos, (one[0] + one[1]) * cos
    if 8 * part == 3 * whole:
        return (one[0] + one[1]) * cos, (one[1] - one[0]) * cos
    return one[0] * cos - one[1] * sin, one[0] * sin + one[1] * cos


def dft4(a, b, c, d):
    even, odd = add(a, c), sub(a, c)
    both, diff = add(b, d), by_i(sub(b, d))
    return [add(even, both), add(odd, diff), sub(even, both), sub(odd, diff)]


def dft8(items):
    even = dft4(*items[0::2])
    odd = dft4(*items[1::2])
    odd = [turn(item, place, 8) for place, item in enumerate(odd)]
    return [add(e, o) for e, o in zip(even, odd)] + [sub(e, o) for e, o in zip(even, odd)]


def dft32(items):
    firsts = []
    for j in range(8):
        four = dft4(items[j], items[j + 8], items[j + 16], items[j + 24])
        firsts.append([turn(item, j * r, 32) for r, item in enumerate(four)])
    out = [None] * 32
    for r in range(4):
        for q, item in enumerate(dft8([firsts[j][r] for j in range(8)])):
            out[r + 4 * q] = item
    return out


def lines_kernel(data, table, matrix, out, wide, flat):
    def columns(index, carry):
        base = index // 2 * 32 + index % 2 * 8
        base_imag = base + 16
        items = []
        for k1 in range(GROUP):
            scale = table[0, k1 : k1 + 1, :]
            items.append(
                (data[k1, pl.ds(base, 8), :] * scale, data[k1, pl.ds(base_imag, 8), :] * scale)
            )
        pair = []
        for m, item in enumerate(dft32(items)):
            cos, sin = table[1, m : m + 1, :], table[2, m : m + 1, :]
            pair.append((item[0] * cos - item[1] * sin, item[0] * sin + item[1] * cos))
            if m % 2 == 1:
                row = index * 256 + m * 8 - 8
                real, imag = [jnp.concatenate(parts, axis=0) for parts in zip(*pair)]
                for at, part in ((0, real), (CELLS, imag)):
                    high, low = split(part)
                    wide[pl.ds(row, 16), at : at + CELLS] = high
                    wide[pl.ds(row, 16), at + 256 : at + 256 + CELLS] = high
                    wide[pl.ds(row, 16), at + 512 : at + 512 + CELLS] = low
                pair = []
        return carry

    for index in range(6):
        columns(index, 0)
    flat[...] = jnp.dot(wide[...], matrix[...], preferred_element_type=jnp.float32)
    lane = lax.broadcasted_iota(jnp.int32, (GROUP, CELLS), 1)
    odd = lane // 32 % 2 == 1
    upper = lane // 64 == 1
    for index in range(6):
        for half in range(2):
            rows = [
                flat[pl.ds(index * 256 + half * 4 + line, GROUP, stride=8), :]
                for line in range(4)
            ]
            turned = jnp.concatenate(rows, axis=0).T
            v = [turned[s * 32 : s * 32 + 32] for s in range(4)]
            w = [
                jnp.where(odd, pltpu.roll(v[1], 32, 1), v[0]),
                jnp.where(odd, v[1], pltpu.roll(v[0], 96, 1)),
                jnp.where(odd, pltpu.roll(v[3], 32, 1), v[2]),
                jnp.where(odd, v[3], pltpu.roll(v[2], 96, 1)),
            ]
            o = [
                jnp.where(upper, pltpu.roll(w[2], 64, 1), w[0]),
                jnp.where(upper, pltpu.roll(w[3], 64, 1), w[1]),
                jnp.where(upper, w[2], pltpu.roll(w[0], 64, 1)),
                jnp.where(upper, w[3], pltpu.roll(w[1], 64, 1)),
            ]
            for line in range(4):
                row = index * 8 + half * 4 + line
                out[pl.ds(row, GROUP, stride=SENT), :] = o[line]
    empty = jnp.zeros((16, CELLS), jnp.float32)
    left = lax.broadcasted_iota(jnp.int32, (GROUP, CELLS), 1) < 64
    for pair in range(3):
        rows = []
        for edge in (2 * pair, 2 * pair + 1):
            m = 29 + edge if edge < 3 else edge - 3
            rows += [flat[index * 256 + m * 8 : index * 256 + m * 8 + 8, :] for index in range(6)]
            rows += [empty]
        turned = jnp.concatenate(rows, axis=0).T
        before = pltpu.roll(turned[96:128], 1, 0)
        after = pltpu.roll(turned[0:32], 31, 0)
        moved = (before, jnp.where(left, before, after), after)[pair]
        out[pl.ds(LINES + pair, GROUP, stride=SENT), :] = moved


def transform(received):
    numbers, matrix = tables()
    return pl.pallas_call(
        lines_kernel,
        out_shape=jax.ShapeDtypeStruct((GROUP * SENT, CELLS), jnp.float32),
        scratch_shapes=[
            pltpu.VMEM((GROUP * LINES, 768), jnp.bfloat16),
            pltpu.VMEM((GROUP * LINES, CELLS), jnp.float32),
        ],
        compiler_params=pltpu.CompilerParams(vmem_limit_bytes=16 * MIB),
        name="lines",
    )(received, jnp.asarray(numbers), jnp.asarray(matrix))


def spline_weights(frac):
    cube = frac * frac * frac
    square = frac * frac
    rest = 1.0 - frac
    return [
        rest * rest * rest / 6.0,
        (3.0 * cube - 6.0 * square + 4.0) / 6.0,
        (-3.0 * cube + 3.0 * square + 3.0 * frac + 1.0) / 6.0,
        cube / 6.0,
    ]


def spread(weights, step):
    out = jnp.where(step == 0, weights[0], 0.0)
    for place in range(1, 4):
        out = jnp.where(step == place, weights[place], out)
    return out


def weights_kernel(lengths, cells, offsets, counts_far, near, side, counts, done):
    copy = pltpu.make_async_copy(counts_far, counts, done)
    copy.start()
    start_y = lax.axis_index("gy") * CELLS
    start_z = lax.axis_index("gz") * CELLS
    row = lax.broadcasted_iota(jnp.int32, (CELLS, TILE), 0)
    row_y = lax.broadcasted_iota(jnp.int32, (CELLS + 16, TILE), 0) - 8
    spot8 = lax.broadcasted_iota(jnp.int32, (8, TILE), 0)
    edge = jnp.where(spot8 < 4, 2 * spot8, 2 * spot8 - 7)
    edge = jnp.where(edge < 3, edge - 3, jnp.where(edge < 6, edge + 125, -9999))
    blank = jnp.zeros((8, TILE), jnp.float32)

    def tile(index, carry):
        spot = pl.ds(pl.multiple_of(index * TILE, TILE), TILE)
        first_y = ((cells[0:1, spot] - start_y + 2) & (lengths[0] - 1)) - 3
        first_z = ((cells[1:2, spot] - start_z + 2) & (lengths[1] - 1)) - 3
        weights = [spline_weights(offsets[d : d + 1, spot]) for d in range(3)]
        high, low = split(spread(weights[2], row - first_z))
        near[index, 0:128, :] = high
        near[index, 128:256, :] = high
        near[index, 256:384, :] = low
        outer = spread(weights[2], edge - first_z)
        coarse = outer.astype(jnp.bfloat16).astype(jnp.float32)
        block = jnp.concatenate([coarse, outer - coarse, coarse, blank], axis=0)
        for part in range(4):
            near[index, 384 + part * 32 : 416 + part * 32, :] = block.astype(jnp.bfloat16)
        side[index, 0:144, :] = spread(weights[1], row_y - first_y)
        side[index, 144:148, :] = jnp.concatenate(weights[0], axis=0)
        return carry

    lax.fori_loop(0, cells.shape[1] // TILE, tile, 0)
    copy.wait()
    lane = lax.broadcasted_iota(jnp.int32, (4, TILE), 1)
    for index in range(cells.shape[1] // TILE):
        live = lane + index * TILE < counts[0]
        side[index, 148:152, :] = jnp.where(live, 1.0, 0.0)


def fill(wide, row, count, inner, outer):
    high, low = split(inner)
    wide[row : row + count, 0:128] = high
    wide[row : row + count, 128:256] = low
    wide[row : row + count, 256:384] = high
    wide[row : row + count, 384:512] = outer.astype(jnp.bfloat16)


def turn_tails(tails):
    row = lax.broadcasted_iota(jnp.int32, (8, CELLS), 0)
    rows = []
    for tail in tails:
        both = jnp.where(row < 4, pltpu.roll(tail, 3, 0), pltpu.roll(tail, 7, 0))
        both = jnp.where(row % 4 == 3, 0.0, both)
        coarse = both.astype(jnp.bfloat16).astype(jnp.float32)
        rows += [coarse, coarse, both - coarse, jnp.zeros_like(both)]
    turned = jnp.concatenate(rows, axis=0).T
    lane = lax.broadcasted_iota(jnp.int32, (64, CELLS), 1)
    return jnp.where(lane % 8 < 4, turned[:64], turned[64:])


def block_kernel(data, near, side, coefficients, sums, wide, held):
    lane = lax.broadcasted_iota(jnp.int32, (LINES, CELLS), 1)
    for group in range(8):
        turned = turn_tails(
            [data[(group * 4 + t + 1) * SENT - 8 : (group * 4 + t + 1) * SENT, :] for t in range(4)]
        )[:LINES]
        for t in range(4):
            whole = group * 4 + t
            inner = data[whole * SENT : whole * SENT + LINES, :]
            fill(wide, whole * LINES, LINES, inner, jnp.where(lane // 32 == t, turned, 0.0))
            for c in range(3):
                coefficients[c, whole // 8, whole % 8 * 16 : whole % 8 * 16 + 16, :] = inner[
                    c * 16 : c * 16 + 16
                ]

    def tile(index, slot):
        held[slot] = jnp.dot(wide[...], near[index], preferred_element_type=jnp.float32)
        totals = [[None] * 3 for _ in range(4)]
        for part in range(16):
            weight = side[index, 8 + part * 8 : 16 + part * 8, :]
            for a in range(4):
                for c in range(3):
                    place = (a * 8 + part // 2) * LINES + c * 16 + part % 2 * 8
                    term = held[slot, place : place + 8, :] * weight
                    total = totals[a][c]
                    totals[a][c] = term if total is None else total + term
        for c in range(3):
            total = totals[0][c] * side[index, 144:145, :]
            for a in range(1, 4):
                total = total + totals[a][c] * side[index, 144 + a : 145 + a, :]
            at = index * TILE
            sums[c : c + 1, at : at + TILE] = jnp.sum(total, axis=0, keepdims=True)

    for index in range(near.shape[0]):
        tile(index, index % 2)


def edge_kernel(above, below, near, side, sums, out, wide, held):
    lane = lax.broadcasted_iota(jnp.int32, (8, CELLS), 1)
    row = lax.broadcasted_iota(jnp.int32, (8, CELLS), 0)
    parts = []
    for group, rows in enumerate((below, above)):
        turned = turn_tails([rows[a * 16 + 8 : a * 16 + 16, :] for a in range(4)])
        for a in range(4):
            first, second = rows[a * 16 : a * 16 + 8, :], rows[a * 16 + 8 : a * 16 + 16, :]
            for c in range(3):
                three = first if c < 2 else second
                used = row < 3
                if group == 0:
                    three, used = pltpu.roll(three, 5 - c % 2 * 3, 0), row >= 5
                elif c == 1:
                    three = pltpu.roll(three, 5, 0)
                inner = jnp.where(used, three, 0.0)
                at = c * 16 + (8 if group == 0 else 0)
                outer = jnp.where(used & (lane // 32 == a), turned[at : at + 8], 0.0)
                parts.append((inner, outer))
    for place in range(0, 24, 2):
        inner, outer = [jnp.concatenate(pair, axis=0) for pair in zip(*parts[place : place + 2])]
        fill(wide, place * 8, 16, inner, outer)
    for index in range(near.shape[0]):
        at = index * TILE
        held[index] = jnp.dot(wide[...], near[index], preferred_element_type=jnp.float32)
        live = side[index, 148:149, :] > 0.5
        low = side[index, 0:8, :]
        high = side[index, 136:144, :]
        for c in range(3):
            total = None
            for a in range(4):
                term = (
                    held[index, (a * 3 + c) * 8 : (a * 3 + c) * 8 + 8, :] * low
                    + held[index, ((a + 4) * 3 + c) * 8 : ((a + 4) * 3 + c) * 8 + 8, :] * high
                ) * side[index, 144 + a : 145 + a, :]
                total = term if total is None else total + term
            value = sums[c : c + 1, at : at + TILE] + jnp.sum(total, axis=0, keepdims=True)
            out[c : c + 1, at : at + TILE] = jnp.where(live, value, 0.0)


def vmem():
    return pl.BlockSpec(memory_space=pltpu.VMEM)


def rims_kernel(data, bottom, top):
    for a in range(4):
        for out, first, low in ((bottom, a * 8 * SENT, 0), (top, (a * 8 + 7) * SENT, 13)):
            rows = [data[first + c * 16 + low : first + c * 16 + low + 3, :] for c in range(3)]
            rows.append(data[first + 46 : first + SENT, :])
            for place, part in zip((0, 3, 8, 11), rows):
                out[a * 16 + place : a * 16 + place + part.shape[0], :] = part
            out[a * 16 + 6 : a * 16 + 8, :] = jnp.zeros((2, CELLS), jnp.float32)


def rims(owned):
    return pl.pallas_call(
        rims_kernel,
        in_specs=[vmem()],
        out_specs=[vmem()] * 2,
        out_shape=[jax.ShapeDtypeStruct((64, CELLS), jnp.float32)] * 2,
        compiler_params=pltpu.CompilerParams(vmem_limit_bytes=4 * MIB),
        name="rims",
    )(owned)


def particle_weights(lengths, cells, offsets, counts):
    def body(*refs):
        weights_kernel(lengths, *refs)

    count = cells.shape[1] // TILE
    return pl.pallas_call(
        body,
        in_specs=[vmem()] * 2 + [pl.BlockSpec(memory_space=pl.ANY)],
        out_specs=[vmem()] * 2,
        out_shape=[
            jax.ShapeDtypeStruct((count, 512, TILE), jnp.bfloat16),
            jax.ShapeDtypeStruct((count, CELLS + 24, TILE), jnp.float32),
        ],
        scratch_shapes=[pltpu.SMEM((1,), jnp.int32), pltpu.SemaphoreType.DMA],
        compiler_params=pltpu.CompilerParams(vmem_limit_bytes=10 * MIB),
        cost_estimate=pl.CostEstimate(
            flops=10_000_000, bytes_accessed=4_000_000, transcendentals=0
        ),
        name="weights",
    )(cells, offsets, counts)


def interpolate_block(data, near, side):
    count = near.shape[0]
    return pl.pallas_call(
        block_kernel,
        in_specs=[vmem()] * 3,
        out_specs=[vmem()] * 2,
        out_shape=[
            jax.ShapeDtypeStruct((3, 4, CELLS, CELLS), jnp.float32),
            jax.ShapeDtypeStruct((3, count * TILE), jnp.float32),
        ],
        scratch_shapes=[
            pltpu.VMEM((GROUP * LINES, 512), jnp.bfloat16),
            pltpu.VMEM((2, GROUP * LINES, TILE), jnp.float32),
        ],
        compiler_params=pltpu.CompilerParams(vmem_limit_bytes=16 * MIB),
        name="block",
    )(data, near, side)


def interpolate_edges(above, below, near, side, sums):
    return pl.pallas_call(
        edge_kernel,
        in_specs=[vmem()] * 5,
        out_specs=vmem(),
        out_shape=jax.ShapeDtypeStruct(sums.shape, jnp.float32),
        scratch_shapes=[
            pltpu.VMEM((192, 512), jnp.bfloat16),
            pltpu.VMEM((near.shape[0], 192, TILE), jnp.float32),
        ],
        compiler_params=pltpu.CompilerParams(vmem_limit_bytes=10 * MIB),
        name="edges",
    )(above, below, near, side, sums)


def per_device(spectrum, cells, offsets, counts):
    rows_y, rows_z = spectrum.shape[3], spectrum.shape[4]
    count_y, count_z = lax.axis_size("gy"), lax.axis_size("gz")
    lengths = (rows_y * count_y, rows_z * count_z)
    by_target = spectrum.reshape(6, GROUP, 16, CELLS).transpose(1, 0, 2, 3)
    received = lax.all_to_all(
        by_target.reshape(GROUP, 96, CELLS), "gz", split_axis=0, concat_axis=0, tiled=True
    )
    lines = transform(received).reshape(GROUP, SENT, 1, CELLS)
    owned = lax.all_to_all(lines, "gz", split_axis=0, concat_axis=0, tiled=True)
    owned = owned.reshape(GROUP * SENT, CELLS)
    bottom, top = rims(owned)
    forward = [(i, (i + 1) % count_y) for i in range(count_y)]
    backward = [(target, source) for source, target in forward]
    above = lax.ppermute(bottom, "gy", backward)
    below = lax.ppermute(top, "gy", forward)
    near, side = particle_weights(lengths, cells, offsets, counts)
    coefficients, sums = interpolate_block(owned, near, side)
    interpolated = interpolate_edges(above, below, near, side, sums)
    return coefficients, interpolated


def solution(mesh):
    placed = (
        P(None, None, None, "gy", "gz"),
        P(None, ("gz", "gy")),
        P(None, ("gz", "gy")),
        P(("gz", "gy")),
    )
    return jax.shard_map(
        per_device,
        mesh=mesh,
        in_specs=placed,
        out_specs=(P(None, None, "gy", "gz"), P(None, ("gz", "gy"))),
        check_vma=False,
    )
```

```python
import math

import jax
import jax.numpy as jnp
import numpy as np
from jax import lax
from jax.experimental import pallas as pl
from jax.experimental.pallas import tpu as pltpu
from jax.sharding import PartitionSpec as P

GROUP = 32
CELLS = 128
LINES = 48
SENT = 51
TILE = 256
MIB = 1024 * 1024
HOPS = 3


def split(value):
    high = value.astype(jnp.bfloat16)
    low = (value - high.astype(jnp.float32)).astype(jnp.bfloat16)
    return high, low


def tables():
    length = GROUP * CELLS
    place = np.arange(length, dtype=np.float64).reshape(GROUP, CELLS)
    symbol = (4.0 + 2.0 * np.cos(2.0 * np.pi * place / length)) / 6.0
    scale = 1.0 / (symbol * math.sqrt(length))
    twist = 2.0 * np.pi * np.outer(np.arange(GROUP), np.arange(CELLS)) / length
    columns = np.arange(CELLS)
    outer = 4 * (columns % GROUP) + columns // GROUP
    last = 2.0 * np.pi * (np.outer(np.arange(CELLS), outer) % CELLS) / CELLS
    matrix = np.concatenate([np.cos(last), -np.sin(last)], axis=0).astype(np.float32)
    high = matrix.astype(jnp.bfloat16)
    low = (matrix - high.astype(np.float32)).astype(jnp.bfloat16)
    return (
        np.stack([scale, np.cos(twist), np.sin(twist)]).astype(np.float32),
        np.concatenate([high, low, high], axis=0),
    )


def add(one, two):
    return one[0] + two[0], one[1] + two[1]


def sub(one, two):
    return one[0] - two[0], one[1] - two[1]


def by_i(one):
    return -one[1], one[0]


def turn(one, part, whole):
    part = part % whole
    if part == 0:
        return one
    if 4 * part == whole:
        return by_i(one)
    if 2 * part == whole:
        return -one[0], -one[1]
    if 4 * part == 3 * whole:
        return one[1], -one[0]
    cos = math.cos(2.0 * math.pi * part / whole)
    sin = math.sin(2.0 * math.pi * part / whole)
    if 8 * part == whole:
        return (one[0] - one[1]) * cos, (one[0] + one[1]) * cos
    if 8 * part == 3 * whole:
        return (one[0] + one[1]) * cos, (one[1] - one[0]) * cos
    return one[0] * cos - one[1] * sin, one[0] * sin + one[1] * cos


def dft4(a, b, c, d):
    even, odd = add(a, c), sub(a, c)
    both, diff = add(b, d), by_i(sub(b, d))
    return [add(even, both), add(odd, diff), sub(even, both), sub(odd, diff)]


def dft8(items):
    even = dft4(*items[0::2])
    odd = dft4(*items[1::2])
    odd = [turn(item, place, 8) for place, item in enumerate(odd)]
    return [add(e, o) for e, o in zip(even, odd)] + [sub(e, o) for e, o in zip(even, odd)]


def lines_kernel(data, table, matrix, out, wide, flat):
    lane = lax.broadcasted_iota(jnp.int32, (GROUP, CELLS), 1)
    odd = lane // 32 % 2 == 1
    upper = lane // 64 == 1

    def firsts_of(index):
        base = index // 2 * 32 + index % 2 * 8

        def item(k1):
            scale = table[0, k1 : k1 + 1, :]
            return data[k1, base : base + 8, :] * scale, data[k1, base + 16 : base + 24, :] * scale

        firsts = []
        for j in range(8):
            four = dft4(*[item(j + 8 * step) for step in range(4)])
            firsts.append([turn(value, j * r, 32) for r, value in enumerate(four)])
        return firsts

    def seconds_of(index, firsts, low):
        both = []
        for r in (low, low + 1):
            values = dft8([firsts[j][r] for j in range(8)])
            turned = []
            for q, value in enumerate(values):
                m = r + 4 * q
                cos, sin = table[1, m : m + 1, :], table[2, m : m + 1, :]
                turned.append((value[0] * cos - value[1] * sin, value[0] * sin + value[1] * cos))
            both.append(turned)
        for q in range(8):
            row = index * 256 + (low + 4 * q) * 8
            for at, half in ((0, 0), (CELLS, 1)):
                part = jnp.concatenate([both[0][q][half], both[1][q][half]], axis=0)
                high, low_part = split(part)
                wide[row : row + 16, at : at + CELLS] = high
                wide[row : row + 16, at + 256 : at + 256 + CELLS] = high
                wide[row : row + 16, at + 512 : at + 512 + CELLS] = low_part

    def place(index, half):
        rows = [
            flat[pl.ds(index * 256 + half * 4 + line, GROUP, stride=8), :] for line in range(4)
        ]
        turned = jnp.concatenate(rows, axis=0).T
        v = [turned[s * 32 : s * 32 + 32] for s in range(4)]
        w = [
            jnp.where(odd, pltpu.roll(v[1], 32, 1), v[0]),
            jnp.where(odd, v[1], pltpu.roll(v[0], 96, 1)),
            jnp.where(odd, pltpu.roll(v[3], 32, 1), v[2]),
            jnp.where(odd, v[3], pltpu.roll(v[2], 96, 1)),
        ]
        o = [
            jnp.where(upper, pltpu.roll(w[2], 64, 1), w[0]),
            jnp.where(upper, pltpu.roll(w[3], 64, 1), w[1]),
            jnp.where(upper, w[2], pltpu.roll(w[0], 64, 1)),
            jnp.where(upper, w[3], pltpu.roll(w[1], 64, 1)),
        ]
        for line in range(4):
            row = index * 8 + half * 4 + line
            out[pl.ds(row, GROUP, stride=SENT), :] = o[line]

    for index in range(6):
        firsts = firsts_of(index)
        if index:
            place(index - 1, 0)
        seconds_of(index, firsts, 0)
        if index:
            place(index - 1, 1)
        seconds_of(index, firsts, 2)
        part = slice(index * 256, index * 256 + 256)
        flat[part, :] = jnp.dot(wide[part, :], matrix[...], preferred_element_type=jnp.float32)
    place(5, 0)
    place(5, 1)
    empty = jnp.zeros((16, CELLS), jnp.float32)
    left = lax.broadcasted_iota(jnp.int32, (GROUP, CELLS), 1) < 64
    for pair in range(3):
        rows = []
        for edge in (2 * pair, 2 * pair + 1):
            m = 29 + edge if edge < 3 else edge - 3
            rows += [flat[index * 256 + m * 8 : index * 256 + m * 8 + 8, :] for index in range(6)]
            rows += [empty]
        turned = jnp.concatenate(rows, axis=0).T
        before = pltpu.roll(turned[96:128], 1, 0)
        after = pltpu.roll(turned[0:32], 31, 0)
        moved = (before, jnp.where(left, before, after), after)[pair]
        out[pl.ds(LINES + pair, GROUP, stride=SENT), :] = moved


def transform(received):
    numbers, matrix = tables()
    return pl.pallas_call(
        lines_kernel,
        out_shape=jax.ShapeDtypeStruct((GROUP * SENT, CELLS), jnp.float32),
        scratch_shapes=[
            pltpu.VMEM((GROUP * LINES, 768), jnp.bfloat16),
            pltpu.VMEM((GROUP * LINES, CELLS), jnp.float32),
        ],
        compiler_params=pltpu.CompilerParams(vmem_limit_bytes=16 * MIB),
        name="lines",
    )(received, jnp.asarray(numbers), jnp.asarray(matrix))


def spline_weights(frac):
    cube = frac * frac * frac
    square = frac * frac
    rest = 1.0 - frac
    return [
        rest * rest * rest / 6.0,
        (3.0 * cube - 6.0 * square + 4.0) / 6.0,
        (-3.0 * cube + 3.0 * square + 3.0 * frac + 1.0) / 6.0,
        cube / 6.0,
    ]


def spread(weights, step):
    out = jnp.where(step == 0, weights[0], 0.0)
    for place in range(1, 4):
        out = jnp.where(step == place, weights[place], out)
    return out


def weights_kernel(lengths, cells, offsets, counts_far, near, side, counts, done):
    copy = pltpu.make_async_copy(counts_far, counts, done)
    copy.start()
    start_y = lax.axis_index("gy") * CELLS
    start_z = lax.axis_index("gz") * CELLS
    row = lax.broadcasted_iota(jnp.int32, (CELLS, TILE), 0)
    row_y = lax.broadcasted_iota(jnp.int32, (CELLS + 16, TILE), 0) - 8
    spot8 = lax.broadcasted_iota(jnp.int32, (8, TILE), 0)
    edge = jnp.where(spot8 < 4, 2 * spot8, 2 * spot8 - 7)
    edge = jnp.where(edge < 3, edge - 3, jnp.where(edge < 6, edge + 125, -9999))
    blank = jnp.zeros((8, TILE), jnp.float32)

    def tile(index, carry):
        spot = pl.ds(pl.multiple_of(index * TILE, TILE), TILE)
        first_y = ((cells[0:1, spot] - start_y + 2) & (lengths[0] - 1)) - 3
        first_z = ((cells[1:2, spot] - start_z + 2) & (lengths[1] - 1)) - 3
        weights = [spline_weights(offsets[d : d + 1, spot]) for d in range(3)]
        high, low = split(spread(weights[2], row - first_z))
        near[index, 0:128, :] = high
        near[index, 128:256, :] = high
        near[index, 256:384, :] = low
        outer = spread(weights[2], edge - first_z)
        coarse = outer.astype(jnp.bfloat16).astype(jnp.float32)
        block = jnp.concatenate([coarse, outer - coarse, coarse, blank], axis=0)
        for part in range(4):
            near[index, 384 + part * 32 : 416 + part * 32, :] = block.astype(jnp.bfloat16)
        side[index, 0:144, :] = spread(weights[1], row_y - first_y)
        side[index, 144:148, :] = jnp.concatenate(weights[0], axis=0)
        return carry

    lax.fori_loop(0, cells.shape[1] // TILE, tile, 0)
    copy.wait()
    lane = lax.broadcasted_iota(jnp.int32, (4, TILE), 1)
    for index in range(cells.shape[1] // TILE):
        live = lane + index * TILE < counts[0]
        side[index, 148:152, :] = jnp.where(live, 1.0, 0.0)


def fill(wide, row, count, inner, outer):
    high, low = split(inner)
    wide[row : row + count, 0:128] = high
    wide[row : row + count, 128:256] = low
    wide[row : row + count, 256:384] = high
    wide[row : row + count, 384:512] = outer.astype(jnp.bfloat16)


def turn_tails(tails):
    row = lax.broadcasted_iota(jnp.int32, (8, CELLS), 0)
    rows = []
    for tail in tails:
        both = jnp.where(row < 4, pltpu.roll(tail, 3, 0), pltpu.roll(tail, 7, 0))
        both = jnp.where(row % 4 == 3, 0.0, both)
        coarse = both.astype(jnp.bfloat16).astype(jnp.float32)
        rows += [coarse, coarse, both - coarse, jnp.zeros_like(both)]
    turned = jnp.concatenate(rows, axis=0).T
    lane = lax.broadcasted_iota(jnp.int32, (64, CELLS), 1)
    return jnp.where(lane % 8 < 4, turned[:64], turned[64:])


def block_kernel(data, near, side, coefficients, sums, wide, held):
    lane = lax.broadcasted_iota(jnp.int32, (LINES, CELLS), 1)
    for group in range(8):
        turned = turn_tails(
            [data[(group * 4 + t + 1) * SENT - 8 : (group * 4 + t + 1) * SENT, :] for t in range(4)]
        )[:LINES]
        for t in range(4):
            whole = group * 4 + t
            inner = data[whole * SENT : whole * SENT + LINES, :]
            fill(wide, whole * LINES, LINES, inner, jnp.where(lane // 32 == t, turned, 0.0))
            for c in range(3):
                coefficients[c, whole // 8, whole % 8 * 16 : whole % 8 * 16 + 16, :] = inner[
                    c * 16 : c * 16 + 16
                ]

    def tile(index, slot):
        held[slot] = jnp.dot(wide[...], near[index], preferred_element_type=jnp.float32)
        totals = [[None] * 3 for _ in range(4)]
        for part in range(16):
            weight = side[index, 8 + part * 8 : 16 + part * 8, :]
            for a in range(4):
                for c in range(3):
                    place = (a * 8 + part // 2) * LINES + c * 16 + part % 2 * 8
                    term = held[slot, place : place + 8, :] * weight
                    total = totals[a][c]
                    totals[a][c] = term if total is None else total + term
        for c in range(3):
            total = totals[0][c] * side[index, 144:145, :]
            for a in range(1, 4):
                total = total + totals[a][c] * side[index, 144 + a : 145 + a, :]
            at = index * TILE
            sums[c : c + 1, at : at + TILE] = jnp.sum(total, axis=0, keepdims=True)

    for index in range(near.shape[0]):
        tile(index, index % 2)


def edge_kernel(above, below, near, side, sums, out, wide, held):
    lane = lax.broadcasted_iota(jnp.int32, (8, CELLS), 1)
    row = lax.broadcasted_iota(jnp.int32, (8, CELLS), 0)
    parts = []
    for group, rows in enumerate((below, above)):
        turned = turn_tails([rows[a * 16 + 8 : a * 16 + 16, :] for a in range(4)])
        for a in range(4):
            first, second = rows[a * 16 : a * 16 + 8, :], rows[a * 16 + 8 : a * 16 + 16, :]
            for c in range(3):
                three = first if c < 2 else second
                used = row < 3
                if group == 0:
                    three, used = pltpu.roll(three, 5 - c % 2 * 3, 0), row >= 5
                elif c == 1:
                    three = pltpu.roll(three, 5, 0)
                inner = jnp.where(used, three, 0.0)
                at = c * 16 + (8 if group == 0 else 0)
                outer = jnp.where(used & (lane // 32 == a), turned[at : at + 8], 0.0)
                parts.append((inner, outer))
    for place in range(0, 24, 2):
        inner, outer = [jnp.concatenate(pair, axis=0) for pair in zip(*parts[place : place + 2])]
        fill(wide, place * 8, 16, inner, outer)
    for index in range(near.shape[0]):
        at = index * TILE
        held[index] = jnp.dot(wide[...], near[index], preferred_element_type=jnp.float32)
        live = side[index, 148:149, :] > 0.5
        low = side[index, 0:8, :]
        high = side[index, 136:144, :]
        for c in range(3):
            total = None
            for a in range(4):
                term = (
                    held[index, (a * 3 + c) * 8 : (a * 3 + c) * 8 + 8, :] * low
                    + held[index, ((a + 4) * 3 + c) * 8 : ((a + 4) * 3 + c) * 8 + 8, :] * high
                ) * side[index, 144 + a : 145 + a, :]
                total = term if total is None else total + term
            value = sums[c : c + 1, at : at + TILE] + jnp.sum(total, axis=0, keepdims=True)
            out[c : c + 1, at : at + TILE] = jnp.where(live, value, 0.0)


def vmem():
    return pl.BlockSpec(memory_space=pltpu.VMEM)


def rims_kernel(data, bottom, top):
    for a in range(4):
        for out, first, low in ((bottom, a * 8 * SENT, 0), (top, (a * 8 + 7) * SENT, 13)):
            rows = [data[first + c * 16 + low : first + c * 16 + low + 3, :] for c in range(3)]
            rows.append(data[first + 46 : first + SENT, :])
            for place, part in zip((0, 3, 8, 11), rows):
                out[a * 16 + place : a * 16 + place + part.shape[0], :] = part
            out[a * 16 + 6 : a * 16 + 8, :] = jnp.zeros((2, CELLS), jnp.float32)


def rims(owned):
    return pl.pallas_call(
        rims_kernel,
        in_specs=[vmem()],
        out_specs=[vmem()] * 2,
        out_shape=[jax.ShapeDtypeStruct((64, CELLS), jnp.float32)] * 2,
        compiler_params=pltpu.CompilerParams(vmem_limit_bytes=4 * MIB),
        name="rims",
    )(owned)


def particle_weights(lengths, cells, offsets, counts):
    def body(*refs):
        weights_kernel(lengths, *refs)

    count = cells.shape[1] // TILE
    return pl.pallas_call(
        body,
        in_specs=[vmem()] * 2 + [pl.BlockSpec(memory_space=pl.ANY)],
        out_specs=[vmem()] * 2,
        out_shape=[
            jax.ShapeDtypeStruct((count, 512, TILE), jnp.bfloat16),
            jax.ShapeDtypeStruct((count, CELLS + 24, TILE), jnp.float32),
        ],
        scratch_shapes=[pltpu.SMEM((1,), jnp.int32), pltpu.SemaphoreType.DMA],
        compiler_params=pltpu.CompilerParams(vmem_limit_bytes=10 * MIB),
        cost_estimate=pl.CostEstimate(
            flops=10_000_000, bytes_accessed=4_000_000, transcendentals=0
        ),
        name="weights",
    )(cells, offsets, counts)


def interpolate_block(data, near, side):
    count = near.shape[0]
    return pl.pallas_call(
        block_kernel,
        in_specs=[vmem()] * 3,
        out_specs=[vmem()] * 2,
        out_shape=[
            jax.ShapeDtypeStruct((3, 4, CELLS, CELLS), jnp.float32),
            jax.ShapeDtypeStruct((3, count * TILE), jnp.float32),
        ],
        scratch_shapes=[
            pltpu.VMEM((GROUP * LINES, 512), jnp.bfloat16),
            pltpu.VMEM((2, GROUP * LINES, TILE), jnp.float32),
        ],
        compiler_params=pltpu.CompilerParams(vmem_limit_bytes=16 * MIB),
        name="block",
    )(data, near, side)


def interpolate_edges(above, below, near, side, sums):
    return pl.pallas_call(
        edge_kernel,
        in_specs=[vmem()] * 5,
        out_specs=vmem(),
        out_shape=jax.ShapeDtypeStruct(sums.shape, jnp.float32),
        scratch_shapes=[
            pltpu.VMEM((192, 512), jnp.bfloat16),
            pltpu.VMEM((near.shape[0], 192, TILE), jnp.float32),
        ],
        compiler_params=pltpu.CompilerParams(vmem_limit_bytes=10 * MIB),
        name="edges",
    )(above, below, near, side, sums)


def wait_for_turn(token):
    count = lax.axis_size("gy")
    token = token[:1, :CELLS]
    for _ in range(HOPS):
        token = lax.ppermute(
            token, "gy", [(i, (i + 2) % count) for i in range(1, count, 2)]
        )
    return token[0, 0]


def per_device(spectrum, cells, offsets, counts):
    rows_y, rows_z = spectrum.shape[3], spectrum.shape[4]
    count_y, count_z = lax.axis_size("gy"), lax.axis_size("gz")
    lengths = (rows_y * count_y, rows_z * count_z)
    by_target = spectrum.reshape(6, GROUP, 16, CELLS).transpose(1, 0, 2, 3)
    turn_of = lax.cond(
        (lax.axis_index("gy") & 1) == 1, wait_for_turn, lambda _: jnp.float32(0.0), offsets
    )
    by_target = jnp.where(turn_of != turn_of, 0.0, by_target)
    received = lax.all_to_all(
        by_target.reshape(GROUP, 96, CELLS), "gz", split_axis=0, concat_axis=0, tiled=True
    )
    lines = transform(received).reshape(GROUP, SENT, 1, CELLS)
    owned = lax.all_to_all(lines, "gz", split_axis=0, concat_axis=0, tiled=True)
    owned = owned.reshape(GROUP * SENT, CELLS)
    bottom, top = rims(owned)
    forward = [(i, (i + 1) % count_y) for i in range(count_y)]
    backward = [(target, source) for source, target in forward]
    above = lax.ppermute(bottom, "gy", backward)
    below = lax.ppermute(top, "gy", forward)
    near, side = particle_weights(lengths, cells, offsets, counts)
    coefficients, sums = interpolate_block(owned, near, side)
    interpolated = interpolate_edges(above, below, near, side, sums)
    return coefficients, interpolated


def solution(mesh):
    placed = (
        P(None, None, None, "gy", "gz"),
        P(None, ("gz", "gy")),
        P(None, ("gz", "gy")),
        P(("gz", "gy")),
    )
    return jax.shard_map(
        per_device,
        mesh=mesh,
        in_specs=placed,
        out_specs=(P(None, None, "gy", "gz"), P(None, ("gz", "gy"))),
        check_vma=False,
    )
```

```python
import math

import jax
import jax.numpy as jnp
import numpy as np
from jax import lax
from jax.experimental import pallas as pl
from jax.experimental.pallas import tpu as pltpu
from jax.sharding import PartitionSpec as P

GROUP = 32
CELLS = 128
LINES = 48
SENT = 51
TILE = 256
MIB = 1024 * 1024
HOPS = 2


def split(value):
    high = value.astype(jnp.bfloat16)
    low = (value - high.astype(jnp.float32)).astype(jnp.bfloat16)
    return high, low


def tables():
    length = GROUP * CELLS
    place = np.arange(length, dtype=np.float64).reshape(GROUP, CELLS)
    symbol = (4.0 + 2.0 * np.cos(2.0 * np.pi * place / length)) / 6.0
    scale = 1.0 / (symbol * math.sqrt(length))
    twist = 2.0 * np.pi * np.outer(np.arange(GROUP), np.arange(CELLS)) / length
    columns = np.arange(CELLS)
    outer = 4 * (columns % GROUP) + columns // GROUP
    last = 2.0 * np.pi * (np.outer(np.arange(CELLS), outer) % CELLS) / CELLS
    matrix = np.concatenate([np.cos(last), -np.sin(last)], axis=0).astype(np.float32)
    high = matrix.astype(jnp.bfloat16)
    low = (matrix - high.astype(np.float32)).astype(jnp.bfloat16)
    return (
        np.stack([scale, np.cos(twist), np.sin(twist)]).astype(np.float32),
        np.concatenate([high, low, high], axis=0),
    )


def add(one, two):
    return one[0] + two[0], one[1] + two[1]


def sub(one, two):
    return one[0] - two[0], one[1] - two[1]


def by_i(one):
    return -one[1], one[0]


def turn(one, part, whole):
    part = part % whole
    if part == 0:
        return one
    if 4 * part == whole:
        return by_i(one)
    if 2 * part == whole:
        return -one[0], -one[1]
    if 4 * part == 3 * whole:
        return one[1], -one[0]
    cos = math.cos(2.0 * math.pi * part / whole)
    sin = math.sin(2.0 * math.pi * part / whole)
    if 8 * part == whole:
        return (one[0] - one[1]) * cos, (one[0] + one[1]) * cos
    if 8 * part == 3 * whole:
        return (one[0] + one[1]) * cos, (one[1] - one[0]) * cos
    return one[0] * cos - one[1] * sin, one[0] * sin + one[1] * cos


def dft4(a, b, c, d):
    even, odd = add(a, c), sub(a, c)
    both, diff = add(b, d), by_i(sub(b, d))
    return [add(even, both), add(odd, diff), sub(even, both), sub(odd, diff)]


def dft8(items):
    even = dft4(*items[0::2])
    odd = dft4(*items[1::2])
    odd = [turn(item, place, 8) for place, item in enumerate(odd)]
    return [add(e, o) for e, o in zip(even, odd)] + [sub(e, o) for e, o in zip(even, odd)]


def lines_kernel(data, table, matrix, out, wide, flat):
    lane = lax.broadcasted_iota(jnp.int32, (GROUP, CELLS), 1)
    odd = lane // 32 % 2 == 1
    upper = lane // 64 == 1

    def firsts_of(index):
        base = index // 2 * 32 + index % 2 * 8

        def item(k1):
            scale = table[0, k1 : k1 + 1, :]
            return data[k1, base : base + 8, :] * scale, data[k1, base + 16 : base + 24, :] * scale

        firsts = []
        for j in range(8):
            four = dft4(*[item(j + 8 * step) for step in range(4)])
            firsts.append([turn(value, j * r, 32) for r, value in enumerate(four)])
        return firsts

    def seconds_of(index, firsts, low):
        both = []
        for r in (low, low + 1):
            values = dft8([firsts[j][r] for j in range(8)])
            turned = []
            for q, value in enumerate(values):
                m = r + 4 * q
                cos, sin = table[1, m : m + 1, :], table[2, m : m + 1, :]
                turned.append((value[0] * cos - value[1] * sin, value[0] * sin + value[1] * cos))
            both.append(turned)
        for q in range(8):
            row = index * 256 + (low + 4 * q) * 8
            for at, half in ((0, 0), (CELLS, 1)):
                part = jnp.concatenate([both[0][q][half], both[1][q][half]], axis=0)
                high, low_part = split(part)
                wide[row : row + 16, at : at + CELLS] = high
                wide[row : row + 16, at + 256 : at + 256 + CELLS] = high
                wide[row : row + 16, at + 512 : at + 512 + CELLS] = low_part

    def place(index, half):
        rows = [
            flat[pl.ds(index * 256 + half * 4 + line, GROUP, stride=8), :] for line in range(4)
        ]
        turned = jnp.concatenate(rows, axis=0).T
        v = [turned[s * 32 : s * 32 + 32] for s in range(4)]
        w = [
            jnp.where(odd, pltpu.roll(v[1], 32, 1), v[0]),
            jnp.where(odd, v[1], pltpu.roll(v[0], 96, 1)),
            jnp.where(odd, pltpu.roll(v[3], 32, 1), v[2]),
            jnp.where(odd, v[3], pltpu.roll(v[2], 96, 1)),
        ]
        o = [
            jnp.where(upper, pltpu.roll(w[2], 64, 1), w[0]),
            jnp.where(upper, pltpu.roll(w[3], 64, 1), w[1]),
            jnp.where(upper, w[2], pltpu.roll(w[0], 64, 1)),
            jnp.where(upper, w[3], pltpu.roll(w[1], 64, 1)),
        ]
        for line in range(4):
            row = index * 8 + half * 4 + line
            out[pl.ds(row, GROUP, stride=SENT), :] = o[line]

    for index in range(6):
        firsts = firsts_of(index)
        if index:
            place(index - 1, 0)
        seconds_of(index, firsts, 0)
        if index:
            place(index - 1, 1)
        seconds_of(index, firsts, 2)
        part = slice(index * 256, index * 256 + 256)
        flat[part, :] = jnp.dot(wide[part, :], matrix[...], preferred_element_type=jnp.float32)
    place(5, 0)
    place(5, 1)
    empty = jnp.zeros((16, CELLS), jnp.float32)
    left = lax.broadcasted_iota(jnp.int32, (GROUP, CELLS), 1) < 64
    for pair in range(3):
        rows = []
        for edge in (2 * pair, 2 * pair + 1):
            m = 29 + edge if edge < 3 else edge - 3
            rows += [flat[index * 256 + m * 8 : index * 256 + m * 8 + 8, :] for index in range(6)]
            rows += [empty]
        turned = jnp.concatenate(rows, axis=0).T
        before = pltpu.roll(turned[96:128], 1, 0)
        after = pltpu.roll(turned[0:32], 31, 0)
        moved = (before, jnp.where(left, before, after), after)[pair]
        out[pl.ds(LINES + pair, GROUP, stride=SENT), :] = moved


def transform(received):
    numbers, matrix = tables()
    return pl.pallas_call(
        lines_kernel,
        out_shape=jax.ShapeDtypeStruct((GROUP * SENT, CELLS), jnp.float32),
        scratch_shapes=[
            pltpu.VMEM((GROUP * LINES, 768), jnp.bfloat16),
            pltpu.VMEM((GROUP * LINES, CELLS), jnp.float32),
        ],
        compiler_params=pltpu.CompilerParams(vmem_limit_bytes=16 * MIB),
        name="lines",
    )(received, jnp.asarray(numbers), jnp.asarray(matrix))


def spline_weights(frac):
    cube = frac * frac * frac
    square = frac * frac
    rest = 1.0 - frac
    return [
        rest * rest * rest / 6.0,
        (3.0 * cube - 6.0 * square + 4.0) / 6.0,
        (-3.0 * cube + 3.0 * square + 3.0 * frac + 1.0) / 6.0,
        cube / 6.0,
    ]


def spread(weights, step):
    out = jnp.where(step == 0, weights[0], 0.0)
    for place in range(1, 4):
        out = jnp.where(step == place, weights[place], out)
    return out


def weights_kernel(lengths, cells, offsets, counts_far, near, side, counts, done):
    copy = pltpu.make_async_copy(counts_far, counts, done)
    copy.start()
    start_y = lax.axis_index("gy") * CELLS
    start_z = lax.axis_index("gz") * CELLS
    row = lax.broadcasted_iota(jnp.int32, (CELLS, TILE), 0)
    row_y = lax.broadcasted_iota(jnp.int32, (CELLS + 16, TILE), 0) - 8
    spot8 = lax.broadcasted_iota(jnp.int32, (8, TILE), 0)
    edge = jnp.where(spot8 < 4, 2 * spot8, 2 * spot8 - 7)
    edge = jnp.where(edge < 3, edge - 3, jnp.where(edge < 6, edge + 125, -9999))
    blank = jnp.zeros((8, TILE), jnp.float32)

    def tile(index, carry):
        spot = pl.ds(pl.multiple_of(index * TILE, TILE), TILE)
        first_y = ((cells[0:1, spot] - start_y + 2) & (lengths[0] - 1)) - 3
        first_z = ((cells[1:2, spot] - start_z + 2) & (lengths[1] - 1)) - 3
        weights = [spline_weights(offsets[d : d + 1, spot]) for d in range(3)]
        high, low = split(spread(weights[2], row - first_z))
        near[index, 0:128, :] = high
        near[index, 128:256, :] = high
        near[index, 256:384, :] = low
        outer = spread(weights[2], edge - first_z)
        coarse = outer.astype(jnp.bfloat16).astype(jnp.float32)
        block = jnp.concatenate([coarse, outer - coarse, coarse, blank], axis=0)
        for part in range(4):
            near[index, 384 + part * 32 : 416 + part * 32, :] = block.astype(jnp.bfloat16)
        side[index, 0:144, :] = spread(weights[1], row_y - first_y)
        side[index, 144:148, :] = jnp.concatenate(weights[0], axis=0)
        return carry

    lax.fori_loop(0, cells.shape[1] // TILE, tile, 0)
    copy.wait()
    lane = lax.broadcasted_iota(jnp.int32, (4, TILE), 1)
    for index in range(cells.shape[1] // TILE):
        live = lane + index * TILE < counts[0]
        side[index, 148:152, :] = jnp.where(live, 1.0, 0.0)


def fill(wide, row, count, inner, outer):
    high, low = split(inner)
    wide[row : row + count, 0:128] = high
    wide[row : row + count, 128:256] = low
    wide[row : row + count, 256:384] = high
    wide[row : row + count, 384:512] = outer.astype(jnp.bfloat16)


def turn_tails(tails):
    row = lax.broadcasted_iota(jnp.int32, (8, CELLS), 0)
    rows = []
    for tail in tails:
        both = jnp.where(row < 4, pltpu.roll(tail, 3, 0), pltpu.roll(tail, 7, 0))
        both = jnp.where(row % 4 == 3, 0.0, both)
        coarse = both.astype(jnp.bfloat16).astype(jnp.float32)
        rows += [coarse, coarse, both - coarse, jnp.zeros_like(both)]
    turned = jnp.concatenate(rows, axis=0).T
    lane = lax.broadcasted_iota(jnp.int32, (64, CELLS), 1)
    return jnp.where(lane % 8 < 4, turned[:64], turned[64:])


def block_kernel(data, near, side, coefficients, sums, wide, held):
    lane = lax.broadcasted_iota(jnp.int32, (LINES, CELLS), 1)
    for group in range(8):
        turned = turn_tails(
            [data[(group * 4 + t + 1) * SENT - 8 : (group * 4 + t + 1) * SENT, :] for t in range(4)]
        )[:LINES]
        for t in range(4):
            whole = group * 4 + t
            inner = data[whole * SENT : whole * SENT + LINES, :]
            fill(wide, whole * LINES, LINES, inner, jnp.where(lane // 32 == t, turned, 0.0))
            for c in range(3):
                coefficients[c, whole // 8, whole % 8 * 16 : whole % 8 * 16 + 16, :] = inner[
                    c * 16 : c * 16 + 16
                ]

    def tile(index, slot):
        held[slot] = jnp.dot(wide[...], near[index], preferred_element_type=jnp.float32)
        totals = [[None] * 3 for _ in range(4)]
        for part in range(16):
            weight = side[index, 8 + part * 8 : 16 + part * 8, :]
            for a in range(4):
                for c in range(3):
                    place = (a * 8 + part // 2) * LINES + c * 16 + part % 2 * 8
                    term = held[slot, place : place + 8, :] * weight
                    total = totals[a][c]
                    totals[a][c] = term if total is None else total + term
        for c in range(3):
            total = totals[0][c] * side[index, 144:145, :]
            for a in range(1, 4):
                total = total + totals[a][c] * side[index, 144 + a : 145 + a, :]
            at = index * TILE
            sums[c : c + 1, at : at + TILE] = jnp.sum(total, axis=0, keepdims=True)

    for index in range(near.shape[0]):
        tile(index, index % 2)


def edge_kernel(above, below, near, side, sums, out, wide, held):
    lane = lax.broadcasted_iota(jnp.int32, (8, CELLS), 1)
    row = lax.broadcasted_iota(jnp.int32, (8, CELLS), 0)
    parts = []
    for group, rows in enumerate((below, above)):
        turned = turn_tails([rows[a * 16 + 8 : a * 16 + 16, :] for a in range(4)])
        for a in range(4):
            first, second = rows[a * 16 : a * 16 + 8, :], rows[a * 16 + 8 : a * 16 + 16, :]
            for c in range(3):
                three = first if c < 2 else second
                used = row < 3
                if group == 0:
                    three, used = pltpu.roll(three, 5 - c % 2 * 3, 0), row >= 5
                elif c == 1:
                    three = pltpu.roll(three, 5, 0)
                inner = jnp.where(used, three, 0.0)
                at = c * 16 + (8 if group == 0 else 0)
                outer = jnp.where(used & (lane // 32 == a), turned[at : at + 8], 0.0)
                parts.append((inner, outer))
    for place in range(0, 24, 2):
        inner, outer = [jnp.concatenate(pair, axis=0) for pair in zip(*parts[place : place + 2])]
        fill(wide, place * 8, 16, inner, outer)
    for index in range(near.shape[0]):
        at = index * TILE
        held[index] = jnp.dot(wide[...], near[index], preferred_element_type=jnp.float32)
        live = side[index, 148:149, :] > 0.5
        low = side[index, 0:8, :]
        high = side[index, 136:144, :]
        for c in range(3):
            total = None
            for a in range(4):
                term = (
                    held[index, (a * 3 + c) * 8 : (a * 3 + c) * 8 + 8, :] * low
                    + held[index, ((a + 4) * 3 + c) * 8 : ((a + 4) * 3 + c) * 8 + 8, :] * high
                ) * side[index, 144 + a : 145 + a, :]
                total = term if total is None else total + term
            value = sums[c : c + 1, at : at + TILE] + jnp.sum(total, axis=0, keepdims=True)
            out[c : c + 1, at : at + TILE] = jnp.where(live, value, 0.0)


def vmem():
    return pl.BlockSpec(memory_space=pltpu.VMEM)


def rims_kernel(data, bottom, top):
    for a in range(4):
        for out, first, low in ((bottom, a * 8 * SENT, 0), (top, (a * 8 + 7) * SENT, 13)):
            rows = [data[first + c * 16 + low : first + c * 16 + low + 3, :] for c in range(3)]
            rows.append(data[first + 46 : first + SENT, :])
            for place, part in zip((0, 3, 8, 11), rows):
                out[a * 16 + place : a * 16 + place + part.shape[0], :] = part
            out[a * 16 + 6 : a * 16 + 8, :] = jnp.zeros((2, CELLS), jnp.float32)


def rims(owned):
    return pl.pallas_call(
        rims_kernel,
        in_specs=[vmem()],
        out_specs=[vmem()] * 2,
        out_shape=[jax.ShapeDtypeStruct((64, CELLS), jnp.float32)] * 2,
        compiler_params=pltpu.CompilerParams(vmem_limit_bytes=4 * MIB),
        name="rims",
    )(owned)


def particle_weights(lengths, cells, offsets, counts):
    def body(*refs):
        weights_kernel(lengths, *refs)

    count = cells.shape[1] // TILE
    return pl.pallas_call(
        body,
        in_specs=[vmem()] * 2 + [pl.BlockSpec(memory_space=pl.ANY)],
        out_specs=[vmem()] * 2,
        out_shape=[
            jax.ShapeDtypeStruct((count, 512, TILE), jnp.bfloat16),
            jax.ShapeDtypeStruct((count, CELLS + 24, TILE), jnp.float32),
        ],
        scratch_shapes=[pltpu.SMEM((1,), jnp.int32), pltpu.SemaphoreType.DMA],
        compiler_params=pltpu.CompilerParams(vmem_limit_bytes=10 * MIB),
        cost_estimate=pl.CostEstimate(
            flops=10_000_000, bytes_accessed=4_000_000, transcendentals=0
        ),
        name="weights",
    )(cells, offsets, counts)


def interpolate_block(data, near, side):
    count = near.shape[0]
    return pl.pallas_call(
        block_kernel,
        in_specs=[vmem()] * 3,
        out_specs=[vmem()] * 2,
        out_shape=[
            jax.ShapeDtypeStruct((3, 4, CELLS, CELLS), jnp.float32),
            jax.ShapeDtypeStruct((3, count * TILE), jnp.float32),
        ],
        scratch_shapes=[
            pltpu.VMEM((GROUP * LINES, 512), jnp.bfloat16),
            pltpu.VMEM((2, GROUP * LINES, TILE), jnp.float32),
        ],
        compiler_params=pltpu.CompilerParams(vmem_limit_bytes=16 * MIB),
        name="block",
    )(data, near, side)


def interpolate_edges(above, below, near, side, sums):
    return pl.pallas_call(
        edge_kernel,
        in_specs=[vmem()] * 5,
        out_specs=vmem(),
        out_shape=jax.ShapeDtypeStruct(sums.shape, jnp.float32),
        scratch_shapes=[
            pltpu.VMEM((192, 512), jnp.bfloat16),
            pltpu.VMEM((near.shape[0], 192, TILE), jnp.float32),
        ],
        compiler_params=pltpu.CompilerParams(vmem_limit_bytes=10 * MIB),
        name="edges",
    )(above, below, near, side, sums)


def wait_for_turn(token):
    count = lax.axis_size("gy")
    token = token[0, 0, 0]
    for _ in range(HOPS):
        token = lax.ppermute(
            token, "gy", [(i, (i + 2) % count) for i in range(1, count, 2)]
        )
    return token[0, 0]


def per_device(spectrum, cells, offsets, counts):
    rows_y, rows_z = spectrum.shape[3], spectrum.shape[4]
    count_y, count_z = lax.axis_size("gy"), lax.axis_size("gz")
    lengths = (rows_y * count_y, rows_z * count_z)
    by_target = spectrum.reshape(6, GROUP, 16, CELLS).transpose(1, 0, 2, 3)
    turn_of = lax.cond(
        (lax.axis_index("gy") & 1) == 1, wait_for_turn, lambda _: jnp.float32(0.0), spectrum
    )
    by_target = jnp.where(turn_of != turn_of, 0.0, by_target)
    received = lax.all_to_all(
        by_target.reshape(GROUP, 96, CELLS), "gz", split_axis=0, concat_axis=0, tiled=True
    )
    lines = transform(received).reshape(GROUP, SENT, 1, CELLS)
    owned = lax.all_to_all(lines, "gz", split_axis=0, concat_axis=0, tiled=True)
    owned = owned.reshape(GROUP * SENT, CELLS)
    bottom, top = rims(owned)
    forward = [(i, (i + 1) % count_y) for i in range(count_y)]
    backward = [(target, source) for source, target in forward]
    above = lax.ppermute(bottom, "gy", backward)
    below = lax.ppermute(top, "gy", forward)
    near, side = particle_weights(lengths, cells, offsets, counts)
    coefficients, sums = interpolate_block(owned, near, side)
    interpolated = interpolate_edges(above, below, near, side, sums)
    return coefficients, interpolated


def solution(mesh):
    placed = (
        P(None, None, None, "gy", "gz"),
        P(None, ("gz", "gy")),
        P(None, ("gz", "gy")),
        P(("gz", "gy")),
    )
    return jax.shard_map(
        per_device,
        mesh=mesh,
        in_specs=placed,
        out_specs=(P(None, None, "gy", "gz"), P(None, ("gz", "gy"))),
        check_vma=False,
    )
```

```python
import math

import jax
import jax.numpy as jnp
import numpy as np
from jax import lax
from jax.experimental import pallas as pl
from jax.experimental.pallas import tpu as pltpu
from jax.sharding import PartitionSpec as P

GROUP = 32
CELLS = 128
LINES = 48
SENT = 51
TILE = 256
MIB = 1024 * 1024
HOPS = 2


def split(value):
    high = value.astype(jnp.bfloat16)
    low = (value - high.astype(jnp.float32)).astype(jnp.bfloat16)
    return high, low


def tables():
    length = GROUP * CELLS
    place = np.arange(length, dtype=np.float64).reshape(GROUP, CELLS)
    symbol = (4.0 + 2.0 * np.cos(2.0 * np.pi * place / length)) / 6.0
    scale = 1.0 / (symbol * math.sqrt(length))
    twist = 2.0 * np.pi * np.outer(np.arange(GROUP), np.arange(CELLS)) / length
    columns = np.arange(CELLS)
    outer = 4 * (columns % GROUP) + columns // GROUP
    last = 2.0 * np.pi * (np.outer(np.arange(CELLS), outer) % CELLS) / CELLS
    matrix = np.concatenate([np.cos(last), -np.sin(last)], axis=0).astype(np.float32)
    high = matrix.astype(jnp.bfloat16)
    low = (matrix - high.astype(np.float32)).astype(jnp.bfloat16)
    return (
        np.stack([scale, np.cos(twist), np.sin(twist)]).astype(np.float32),
        np.concatenate([high, low, high], axis=0),
    )


def add(one, two):
    return one[0] + two[0], one[1] + two[1]


def sub(one, two):
    return one[0] - two[0], one[1] - two[1]


def by_i(one):
    return -one[1], one[0]


def turn(one, part, whole):
    part = part % whole
    if part == 0:
        return one
    if 4 * part == whole:
        return by_i(one)
    if 2 * part == whole:
        return -one[0], -one[1]
    if 4 * part == 3 * whole:
        return one[1], -one[0]
    cos = math.cos(2.0 * math.pi * part / whole)
    sin = math.sin(2.0 * math.pi * part / whole)
    if 8 * part == whole:
        return (one[0] - one[1]) * cos, (one[0] + one[1]) * cos
    if 8 * part == 3 * whole:
        return (one[0] + one[1]) * cos, (one[1] - one[0]) * cos
    return one[0] * cos - one[1] * sin, one[0] * sin + one[1] * cos


def dft4(a, b, c, d):
    even, odd = add(a, c), sub(a, c)
    both, diff = add(b, d), by_i(sub(b, d))
    return [add(even, both), add(odd, diff), sub(even, both), sub(odd, diff)]


def dft8(items):
    even = dft4(*items[0::2])
    odd = dft4(*items[1::2])
    odd = [turn(item, place, 8) for place, item in enumerate(odd)]
    return [add(e, o) for e, o in zip(even, odd)] + [sub(e, o) for e, o in zip(even, odd)]


def lines_kernel(data, table, matrix, out, wide, flat):
    lane = lax.broadcasted_iota(jnp.int32, (GROUP, CELLS), 1)
    odd = lane // 32 % 2 == 1
    upper = lane // 64 == 1

    def firsts_of(index):
        base = index // 2 * 32 + index % 2 * 8

        def item(k1):
            scale = table[0, k1 : k1 + 1, :]
            return data[k1, base : base + 8, :] * scale, data[k1, base + 16 : base + 24, :] * scale

        firsts = []
        for j in range(8):
            four = dft4(*[item(j + 8 * step) for step in range(4)])
            firsts.append([turn(value, j * r, 32) for r, value in enumerate(four)])
        return firsts

    def seconds_of(index, firsts, low):
        both = []
        for r in (low, low + 1):
            values = dft8([firsts[j][r] for j in range(8)])
            turned = []
            for q, value in enumerate(values):
                m = r + 4 * q
                cos, sin = table[1, m : m + 1, :], table[2, m : m + 1, :]
                turned.append((value[0] * cos - value[1] * sin, value[0] * sin + value[1] * cos))
            both.append(turned)
        for q in range(8):
            row = index * 256 + (low + 4 * q) * 8
            for at, half in ((0, 0), (CELLS, 1)):
                part = jnp.concatenate([both[0][q][half], both[1][q][half]], axis=0)
                high, low_part = split(part)
                wide[row : row + 16, at : at + CELLS] = high
                wide[row : row + 16, at + 256 : at + 256 + CELLS] = high
                wide[row : row + 16, at + 512 : at + 512 + CELLS] = low_part

    def place(index, half):
        rows = [
            flat[pl.ds(index * 256 + half * 4 + line, GROUP, stride=8), :] for line in range(4)
        ]
        turned = jnp.concatenate(rows, axis=0).T
        v = [turned[s * 32 : s * 32 + 32] for s in range(4)]
        w = [
            jnp.where(odd, pltpu.roll(v[1], 32, 1), v[0]),
            jnp.where(odd, v[1], pltpu.roll(v[0], 96, 1)),
            jnp.where(odd, pltpu.roll(v[3], 32, 1), v[2]),
            jnp.where(odd, v[3], pltpu.roll(v[2], 96, 1)),
        ]
        o = [
            jnp.where(upper, pltpu.roll(w[2], 64, 1), w[0]),
            jnp.where(upper, pltpu.roll(w[3], 64, 1), w[1]),
            jnp.where(upper, w[2], pltpu.roll(w[0], 64, 1)),
            jnp.where(upper, w[3], pltpu.roll(w[1], 64, 1)),
        ]
        for line in range(4):
            row = index * 8 + half * 4 + line
            out[pl.ds(row, GROUP, stride=SENT), :] = o[line]

    for index in range(6):
        firsts = firsts_of(index)
        if index:
            place(index - 1, 0)
        seconds_of(index, firsts, 0)
        if index:
            place(index - 1, 1)
        seconds_of(index, firsts, 2)
        part = slice(index * 256, index * 256 + 256)
        flat[part, :] = jnp.dot(wide[part, :], matrix[...], preferred_element_type=jnp.float32)
    place(5, 0)
    place(5, 1)
    empty = jnp.zeros((16, CELLS), jnp.float32)
    left = lax.broadcasted_iota(jnp.int32, (GROUP, CELLS), 1) < 64
    for pair in range(3):
        rows = []
        for edge in (2 * pair, 2 * pair + 1):
            m = 29 + edge if edge < 3 else edge - 3
            rows += [flat[index * 256 + m * 8 : index * 256 + m * 8 + 8, :] for index in range(6)]
            rows += [empty]
        turned = jnp.concatenate(rows, axis=0).T
        before = pltpu.roll(turned[96:128], 1, 0)
        after = pltpu.roll(turned[0:32], 31, 0)
        moved = (before, jnp.where(left, before, after), after)[pair]
        out[pl.ds(LINES + pair, GROUP, stride=SENT), :] = moved


def transform(received):
    numbers, matrix = tables()
    return pl.pallas_call(
        lines_kernel,
        out_shape=jax.ShapeDtypeStruct((GROUP * SENT, CELLS), jnp.float32),
        scratch_shapes=[
            pltpu.VMEM((GROUP * LINES, 768), jnp.bfloat16),
            pltpu.VMEM((GROUP * LINES, CELLS), jnp.float32),
        ],
        compiler_params=pltpu.CompilerParams(vmem_limit_bytes=16 * MIB),
        name="lines",
    )(received, jnp.asarray(numbers), jnp.asarray(matrix))


def spline_weights(frac):
    cube = frac * frac * frac
    square = frac * frac
    rest = 1.0 - frac
    return [
        rest * rest * rest / 6.0,
        (3.0 * cube - 6.0 * square + 4.0) / 6.0,
        (-3.0 * cube + 3.0 * square + 3.0 * frac + 1.0) / 6.0,
        cube / 6.0,
    ]


def spread(weights, step):
    out = jnp.where(step == 0, weights[0], 0.0)
    for place in range(1, 4):
        out = jnp.where(step == place, weights[place], out)
    return out


def weights_kernel(lengths, cells, offsets, counts_far, near, side, counts, done):
    copy = pltpu.make_async_copy(counts_far, counts, done)
    copy.start()
    start_y = lax.axis_index("gy") * CELLS
    start_z = lax.axis_index("gz") * CELLS
    row = lax.broadcasted_iota(jnp.int32, (CELLS, TILE), 0)
    row_y = lax.broadcasted_iota(jnp.int32, (CELLS + 16, TILE), 0) - 8
    spot8 = lax.broadcasted_iota(jnp.int32, (8, TILE), 0)
    edge = jnp.where(spot8 < 4, 2 * spot8, 2 * spot8 - 7)
    edge = jnp.where(edge < 3, edge - 3, jnp.where(edge < 6, edge + 125, -9999))
    blank = jnp.zeros((8, TILE), jnp.float32)

    def tile(index, carry):
        spot = pl.ds(pl.multiple_of(index * TILE, TILE), TILE)
        first_y = ((cells[0:1, spot] - start_y + 2) & (lengths[0] - 1)) - 3
        first_z = ((cells[1:2, spot] - start_z + 2) & (lengths[1] - 1)) - 3
        weights = [spline_weights(offsets[d : d + 1, spot]) for d in range(3)]
        high, low = split(spread(weights[2], row - first_z))
        near[index, 0:128, :] = high
        near[index, 128:256, :] = high
        near[index, 256:384, :] = low
        outer = spread(weights[2], edge - first_z)
        coarse = outer.astype(jnp.bfloat16).astype(jnp.float32)
        block = jnp.concatenate([coarse, outer - coarse, coarse, blank], axis=0)
        for part in range(4):
            near[index, 384 + part * 32 : 416 + part * 32, :] = block.astype(jnp.bfloat16)
        side[index, 0:144, :] = spread(weights[1], row_y - first_y)
        side[index, 144:148, :] = jnp.concatenate(weights[0], axis=0)
        return carry

    lax.fori_loop(0, cells.shape[1] // TILE, tile, 0)
    copy.wait()
    lane = lax.broadcasted_iota(jnp.int32, (4, TILE), 1)
    for index in range(cells.shape[1] // TILE):
        live = lane + index * TILE < counts[0]
        side[index, 148:152, :] = jnp.where(live, 1.0, 0.0)


def fill(wide, row, count, inner, outer):
    high, low = split(inner)
    wide[row : row + count, 0:128] = high
    wide[row : row + count, 128:256] = low
    wide[row : row + count, 256:384] = high
    wide[row : row + count, 384:512] = outer.astype(jnp.bfloat16)


def turn_tails(tails):
    row = lax.broadcasted_iota(jnp.int32, (8, CELLS), 0)
    rows = []
    for tail in tails:
        both = jnp.where(row < 4, pltpu.roll(tail, 3, 0), pltpu.roll(tail, 7, 0))
        both = jnp.where(row % 4 == 3, 0.0, both)
        coarse = both.astype(jnp.bfloat16).astype(jnp.float32)
        rows += [coarse, coarse, both - coarse, jnp.zeros_like(both)]
    turned = jnp.concatenate(rows, axis=0).T
    lane = lax.broadcasted_iota(jnp.int32, (64, CELLS), 1)
    return jnp.where(lane % 8 < 4, turned[:64], turned[64:])


def block_kernel(data, near, side, coefficients, sums, wide, held):
    lane = lax.broadcasted_iota(jnp.int32, (LINES, CELLS), 1)
    for group in range(8):
        turned = turn_tails(
            [data[(group * 4 + t + 1) * SENT - 8 : (group * 4 + t + 1) * SENT, :] for t in range(4)]
        )[:LINES]
        for t in range(4):
            whole = group * 4 + t
            inner = data[whole * SENT : whole * SENT + LINES, :]
            fill(wide, whole * LINES, LINES, inner, jnp.where(lane // 32 == t, turned, 0.0))
            for c in range(3):
                coefficients[c, whole // 8, whole % 8 * 16 : whole % 8 * 16 + 16, :] = inner[
                    c * 16 : c * 16 + 16
                ]

    def tile(index, slot):
        held[slot] = jnp.dot(wide[...], near[index], preferred_element_type=jnp.float32)
        totals = [[None] * 3 for _ in range(4)]
        for part in range(16):
            weight = side[index, 8 + part * 8 : 16 + part * 8, :]
            for a in range(4):
                for c in range(3):
                    place = (a * 8 + part // 2) * LINES + c * 16 + part % 2 * 8
                    term = held[slot, place : place + 8, :] * weight
                    total = totals[a][c]
                    totals[a][c] = term if total is None else total + term
        for c in range(3):
            total = totals[0][c] * side[index, 144:145, :]
            for a in range(1, 4):
                total = total + totals[a][c] * side[index, 144 + a : 145 + a, :]
            at = index * TILE
            sums[c : c + 1, at : at + TILE] = jnp.sum(total, axis=0, keepdims=True)

    for index in range(near.shape[0]):
        tile(index, index % 2)


def edge_kernel(above, below, near, side, sums, out, wide, held):
    lane = lax.broadcasted_iota(jnp.int32, (8, CELLS), 1)
    row = lax.broadcasted_iota(jnp.int32, (8, CELLS), 0)
    parts = []
    for group, rows in enumerate((below, above)):
        turned = turn_tails([rows[a * 16 + 8 : a * 16 + 16, :] for a in range(4)])
        for a in range(4):
            first, second = rows[a * 16 : a * 16 + 8, :], rows[a * 16 + 8 : a * 16 + 16, :]
            for c in range(3):
                three = first if c < 2 else second
                used = row < 3
                if group == 0:
                    three, used = pltpu.roll(three, 5 - c % 2 * 3, 0), row >= 5
                elif c == 1:
                    three = pltpu.roll(three, 5, 0)
                inner = jnp.where(used, three, 0.0)
                at = c * 16 + (8 if group == 0 else 0)
                outer = jnp.where(used & (lane // 32 == a), turned[at : at + 8], 0.0)
                parts.append((inner, outer))
    for place in range(0, 24, 2):
        inner, outer = [jnp.concatenate(pair, axis=0) for pair in zip(*parts[place : place + 2])]
        fill(wide, place * 8, 16, inner, outer)
    for index in range(near.shape[0]):
        at = index * TILE
        held[index] = jnp.dot(wide[...], near[index], preferred_element_type=jnp.float32)
        live = side[index, 148:149, :] > 0.5
        low = side[index, 0:8, :]
        high = side[index, 136:144, :]
        for c in range(3):
            total = None
            for a in range(4):
                term = (
                    held[index, (a * 3 + c) * 8 : (a * 3 + c) * 8 + 8, :] * low
                    + held[index, ((a + 4) * 3 + c) * 8 : ((a + 4) * 3 + c) * 8 + 8, :] * high
                ) * side[index, 144 + a : 145 + a, :]
                total = term if total is None else total + term
            value = sums[c : c + 1, at : at + TILE] + jnp.sum(total, axis=0, keepdims=True)
            out[c : c + 1, at : at + TILE] = jnp.where(live, value, 0.0)


def vmem():
    return pl.BlockSpec(memory_space=pltpu.VMEM)


def rims_kernel(data, bottom, top):
    for a in range(4):
        for out, first, low in ((bottom, a * 8 * SENT, 0), (top, (a * 8 + 7) * SENT, 13)):
            rows = [data[first + c * 16 + low : first + c * 16 + low + 3, :] for c in range(3)]
            rows.append(data[first + 46 : first + SENT, :])
            for place, part in zip((0, 3, 8, 11), rows):
                out[a * 16 + place : a * 16 + place + part.shape[0], :] = part
            out[a * 16 + 6 : a * 16 + 8, :] = jnp.zeros((2, CELLS), jnp.float32)


def rims(owned):
    return pl.pallas_call(
        rims_kernel,
        in_specs=[vmem()],
        out_specs=[vmem()] * 2,
        out_shape=[jax.ShapeDtypeStruct((64, CELLS), jnp.float32)] * 2,
        compiler_params=pltpu.CompilerParams(vmem_limit_bytes=4 * MIB),
        name="rims",
    )(owned)


def particle_weights(lengths, cells, offsets, counts):
    def body(*refs):
        weights_kernel(lengths, *refs)

    count = cells.shape[1] // TILE
    return pl.pallas_call(
        body,
        in_specs=[vmem()] * 2 + [pl.BlockSpec(memory_space=pl.ANY)],
        out_specs=[vmem()] * 2,
        out_shape=[
            jax.ShapeDtypeStruct((count, 512, TILE), jnp.bfloat16),
            jax.ShapeDtypeStruct((count, CELLS + 24, TILE), jnp.float32),
        ],
        scratch_shapes=[pltpu.SMEM((1,), jnp.int32), pltpu.SemaphoreType.DMA],
        compiler_params=pltpu.CompilerParams(vmem_limit_bytes=10 * MIB),
        cost_estimate=pl.CostEstimate(
            flops=10_000_000, bytes_accessed=4_000_000, transcendentals=0
        ),
        name="weights",
    )(cells, offsets, counts)


def interpolate_block(data, near, side):
    count = near.shape[0]
    return pl.pallas_call(
        block_kernel,
        in_specs=[vmem()] * 3,
        out_specs=[vmem()] * 2,
        out_shape=[
            jax.ShapeDtypeStruct((3, 4, CELLS, CELLS), jnp.float32),
            jax.ShapeDtypeStruct((3, count * TILE), jnp.float32),
        ],
        scratch_shapes=[
            pltpu.VMEM((GROUP * LINES, 512), jnp.bfloat16),
            pltpu.VMEM((2, GROUP * LINES, TILE), jnp.float32),
        ],
        compiler_params=pltpu.CompilerParams(vmem_limit_bytes=16 * MIB),
        name="block",
    )(data, near, side)


def interpolate_edges(above, below, near, side, sums):
    return pl.pallas_call(
        edge_kernel,
        in_specs=[vmem()] * 5,
        out_specs=vmem(),
        out_shape=jax.ShapeDtypeStruct(sums.shape, jnp.float32),
        scratch_shapes=[
            pltpu.VMEM((192, 512), jnp.bfloat16),
            pltpu.VMEM((near.shape[0], 192, TILE), jnp.float32),
        ],
        compiler_params=pltpu.CompilerParams(vmem_limit_bytes=10 * MIB),
        name="edges",
    )(above, below, near, side, sums)


def wait_for_turn(token):
    count = lax.axis_size("gy")
    token = token[0, 0, 0, :96]
    for _ in range(HOPS):
        token = lax.ppermute(
            token, "gy", [(i, (i + 2) % count) for i in range(1, count, 2)]
        )
    return token[0, 0]


def per_device(spectrum, cells, offsets, counts):
    rows_y, rows_z = spectrum.shape[3], spectrum.shape[4]
    count_y, count_z = lax.axis_size("gy"), lax.axis_size("gz")
    lengths = (rows_y * count_y, rows_z * count_z)
    by_target = spectrum.reshape(6, GROUP, 16, CELLS).transpose(1, 0, 2, 3)
    turn_of = lax.cond(
        (lax.axis_index("gy") & 1) == 1, wait_for_turn, lambda _: jnp.float32(0.0), spectrum
    )
    by_target = jnp.where(turn_of != turn_of, 0.0, by_target)
    received = lax.all_to_all(
        by_target.reshape(GROUP, 96, CELLS), "gz", split_axis=0, concat_axis=0, tiled=True
    )
    lines = transform(received).reshape(GROUP, SENT, 1, CELLS)
    owned = lax.all_to_all(lines, "gz", split_axis=0, concat_axis=0, tiled=True)
    owned = owned.reshape(GROUP * SENT, CELLS)
    bottom, top = rims(owned)
    forward = [(i, (i + 1) % count_y) for i in range(count_y)]
    backward = [(target, source) for source, target in forward]
    above = lax.ppermute(bottom, "gy", backward)
    below = lax.ppermute(top, "gy", forward)
    near, side = particle_weights(lengths, cells, offsets, counts)
    coefficients, sums = interpolate_block(owned, near, side)
    interpolated = interpolate_edges(above, below, near, side, sums)
    return coefficients, interpolated


def solution(mesh):
    placed = (
        P(None, None, None, "gy", "gz"),
        P(None, ("gz", "gy")),
        P(None, ("gz", "gy")),
        P(("gz", "gy")),
    )
    return jax.shard_map(
        per_device,
        mesh=mesh,
        in_specs=placed,
        out_specs=(P(None, None, "gy", "gz"), P(None, ("gz", "gy"))),
        check_vma=False,
    )
```
